32 devices in a mesh: page: 8 (over z, x), feat: 4 (over y, core).
Axes of the slice: x: 2, y: 2, z: 4, core: 2. Of those that a mesh axis runs over, the one named last changes fastest.
Arguments:
- queries: bfloat16 [64, 4096], P('page', 'feat')
- fresh_token_keys: bfloat16 [64, 2048], P('page', 'feat')
- fresh_token_values: bfloat16 [64, 2048], P('page', 'feat'), may hold values from -6 to 6
- paged_keys: bfloat16 [128, 256, 2048], P('page', None, 'feat'), may hold values from -6 to 6
- paged_values: bfloat16 [128, 256, 2048], P('page', None, 'feat'), may hold values from -6 to 6
- block_tables: int32 [64, 8], replicated, may hold values from -1 to 127, as said below
- parents: int32 [64], replicated, may hold values from 0 to 63, as said below
- prompt_lengths: int32 [8], replicated, may hold values from 1 to 2047, as said below
- stream: bfloat16 [64, 4608], P(('page', 'feat'))
- output_matrix: bfloat16 [4608, 4096], P(None, 'feat')
- attention_gain: bfloat16 [4608], replicated, may hold values from 0.5 to 1.5
- feedforward_gain: bfloat16 [4608], replicated, may hold values from 0.5 to 1.5
- gate_matrix: bfloat16 [36864, 4608], P(('page', 'feat')), may hold values from -0.09375 to 0.09375
- linear_matrix: bfloat16 [36864, 4608], P(('page', 'feat')), may hold values from -0.09375 to 0.09375
- down_matrix: bfloat16 [36864, 4608], P(('page', 'feat'))
- closing_gain: bfloat16 [4608], replicated, may hold values from 0.5 to 1.5
Outputs:
- layer_output: bfloat16 [64, 4608], P(('page', 'feat'))
The draws below stay inside these ranges and needn't reach their ends.
Inputs may be any that keep to these rules, and one draw needn't show every extreme that they name: `block_tables`: row r's table lists the page slots of its blocks in order; entries from ceil(prompt_lengths[r // 8] / 256) on are -1. Rows of one prompt list the same slots for all but their last listed block, which is each row's own. A slot is listed by the rows of one prompt only, and at most once in a row. `prompt_lengths`: the new token of each prompt's rows stands at this position. `parents`: the parent of row r is a row of the same prompt, from 8 * (r // 8) to that plus 8 - 1.
All inputs are finite; a program needn't handle non-finite values.
Results may differ from the reference program's by a relative error of at most 0.0095.
Values may be sent and summed in bfloat16 or wider, within the bound.
A program may use at most 128 MiB of HBM per device.

```python
import math
import jax
import jax.numpy as jnp
from jax import lax

D = 4608
FF = 36864
QUERY_HEADS = 32
KEY_VALUE_HEADS = 16
HEAD_DIM_SIZE = 128
QSCALAR = 144
SOFTCAP = 50
PAGE_TOKENS = 256
TABLE_BLOCKS = 8
BEAMS = 8
PAGE_SLOTS = 128
PROMPTS = 8
BEAM_ROW_COUNT = 64


def table_entries(key, shape):
    return jax.random.normal(key, shape, jnp.float32)


def spread(key, count):
    uniform_part = jax.random.uniform(key, (count,), jnp.float32)
    return jnp.exp(math.log(6.0) * (uniform_part - 0.5))


def draw_stream(key, part):
    random_subkeys = jax.random.split(jax.random.fold_in(key, 21), 3)
    columns = spread(random_subkeys[0], D)
    row_scale = spread(random_subkeys[1], BEAM_ROW_COUNT)
    values = table_entries(random_subkeys[2], (BEAM_ROW_COUNT, D)) * row_scale[:, None]
    return (values * columns[None, :]).astype(jnp.bfloat16)


def draw_output_matrix(key, part):
    random_subkeys = jax.random.split(jax.random.fold_in(key, 41), 2)
    features = spread(random_subkeys[0], D)
    values = table_entries(random_subkeys[1], (D, QUERY_HEADS * HEAD_DIM_SIZE)) * features[:, None] / math.sqrt(QUERY_HEADS * HEAD_DIM_SIZE)
    return values.astype(jnp.bfloat16)


def draw_down_matrix(key, part):
    random_subkeys = jax.random.split(jax.random.fold_in(key, 51), 2)
    features = spread(random_subkeys[0], D)
    values = table_entries(random_subkeys[1], (FF, D)) * features[None, :] / math.sqrt(FF)
    return values.astype(jnp.bfloat16)


def query_draws(key):
    random_subkeys = jax.random.split(jax.random.fold_in(key, 31), 2)
    softmax_weight = 0.5
    query_vectors = table_entries(random_subkeys[0], (BEAM_ROW_COUNT, QUERY_HEADS * HEAD_DIM_SIZE))
    weighted_total = query_vectors.reshape(BEAM_ROW_COUNT, KEY_VALUE_HEADS, QUERY_HEADS // KEY_VALUE_HEADS, HEAD_DIM_SIZE).sum(axis=2)
    gathered_keys = softmax_weight * weighted_total + 0.5 * table_entries(random_subkeys[1], (BEAM_ROW_COUNT, KEY_VALUE_HEADS, HEAD_DIM_SIZE))
    return (query_vectors, gathered_keys.reshape(BEAM_ROW_COUNT, KEY_VALUE_HEADS * HEAD_DIM_SIZE))


def draw_queries(key, part):
    return query_draws(key)[0].astype(jnp.bfloat16)


def draw_fresh_token_keys(key, part):
    return query_draws(key)[1].astype(jnp.bfloat16)


def page_plan(key):
    random_subkeys = jax.random.split(jax.random.fold_in(key, 7), 5)
    longest = TABLE_BLOCKS * PAGE_TOKENS - 1
    lengths = jax.random.randint(random_subkeys[0], (PROMPTS,), 1, longest + 1)
    long_one = jax.random.randint(random_subkeys[1], (), 0, PROMPTS)
    short_one = (long_one + 1 + jax.random.randint(random_subkeys[2], (), 0, PROMPTS - 1)) % PROMPTS
    prompt_index = jnp.arange(PROMPTS, dtype=jnp.int32)
    lengths = jnp.where(prompt_index == long_one, longest, jnp.where(prompt_index == short_one, 1, lengths))
    stride = TABLE_BLOCKS - 1 + BEAMS
    page_order = jax.random.permutation(random_subkeys[3], PAGE_SLOTS).astype(jnp.int32)
    chosen = jax.random.randint(random_subkeys[4], (), 0, PROMPTS * BEAMS)
    target = chosen // BEAMS * stride + TABLE_BLOCKS - 1 + chosen % BEAMS
    top_spot = jnp.sum(jnp.where(page_order == PAGE_SLOTS - 1, jnp.arange(PAGE_SLOTS, dtype=jnp.int32), 0))
    page_order = page_order.at[top_spot].set(page_order[target]).at[target].set(PAGE_SLOTS - 1)
    row_index = jnp.arange(BEAM_ROW_COUNT, dtype=jnp.int32)
    prompt_of = row_index // BEAMS
    beam_of = row_index % BEAMS
    column = jnp.arange(TABLE_BLOCKS, dtype=jnp.int32)[None, :]
    blocks = ((lengths + PAGE_TOKENS - 1) // PAGE_TOKENS)[prompt_of][:, None]
    shared_at = prompt_of[:, None] * stride + column
    own_at = prompt_of[:, None] * stride + TABLE_BLOCKS - 1 + beam_of[:, None]
    tables = jnp.where(column < blocks - 1, page_order[shared_at], jnp.where(column == blocks - 1, page_order[own_at], -1))
    return (lengths.astype(jnp.int32), tables.astype(jnp.int32))


def draw_prompt_lengths(key, part):
    return page_plan(key)[0]


def draw_block_tables(key, part):
    return page_plan(key)[1]


def draw_parents(key, part):
    row_index = jnp.arange(BEAM_ROW_COUNT, dtype=jnp.int32)
    picks = jax.random.randint(jax.random.fold_in(key, 11), (BEAM_ROW_COUNT,), 0, BEAMS)
    picks = picks.at[0].set(0).at[BEAM_ROW_COUNT - 1].set(BEAMS - 1)
    return (row_index // BEAMS * BEAMS + picks).astype(jnp.int32)


def block_scale(rng, extent, cuts, smallest, largest):
    gain, own = 1.0, jax.random.fold_in(rng, 6)
    for position, shards_of in cuts:
        steps = jnp.exp(jax.random.uniform(jax.random.fold_in(own, position), (shards_of,), jnp.float32, smallest / len(cuts), largest / len(cuts)))
        gain = gain * jnp.repeat(steps, extent[position] // shards_of).reshape([-1 if axis == position else 1 for axis in range(len(extent))])
    return gain


def gaussian(rng, shape, deviation, most, cuts=(), held_as=jnp.bfloat16):
    loudness = block_scale(rng, shape, cuts, -0.22, 0.18) if cuts else 1.0
    values = jax.random.normal(rng, shape, jnp.float32) * deviation * loudness
    return jnp.minimum(jnp.maximum(values, -most), most).astype(held_as)


def setup_inputs(seed: int = 0) -> dict:
    seeds = jax.random.split(jax.random.key(seed), 17)
    return {
        "queries": draw_queries(jax.random.fold_in(seeds[16], 71), 0),
        "fresh_token_keys": draw_fresh_token_keys(jax.random.fold_in(seeds[16], 71), 0),
        "fresh_token_values": gaussian(seeds[2], (BEAM_ROW_COUNT, KEY_VALUE_HEADS * HEAD_DIM_SIZE), 1.0, 6.0, ((0, 8), (1, 4))),
        "paged_keys": gaussian(seeds[3], (PAGE_SLOTS, PAGE_TOKENS, KEY_VALUE_HEADS * HEAD_DIM_SIZE), 1.0, 6.0, ((0, 8), (2, 4))),
        "paged_values": gaussian(seeds[4], (PAGE_SLOTS, PAGE_TOKENS, KEY_VALUE_HEADS * HEAD_DIM_SIZE), 1.0, 6.0, ((0, 8), (2, 4))),
        "block_tables": draw_block_tables(jax.random.fold_in(seeds[16], 71), 0),
        "parents": draw_parents(jax.random.fold_in(seeds[16], 71), 0),
        "prompt_lengths": draw_prompt_lengths(jax.random.fold_in(seeds[16], 71), 0),
        "stream": draw_stream(jax.random.fold_in(seeds[16], 71), 0),
        "output_matrix": draw_output_matrix(jax.random.fold_in(seeds[16], 71), 0),
        "attention_gain": jnp.clip(1.0 + 0.1 * jax.random.normal(seeds[10], (D,), jnp.float32), 0.5, 1.5).astype(jnp.bfloat16),
        "feedforward_gain": jnp.clip(1.0 + 0.1 * jax.random.normal(seeds[11], (D,), jnp.float32), 0.5, 1.5).astype(jnp.bfloat16),
        "gate_matrix": gaussian(seeds[12], (FF, D), D ** -0.5, 0.09375, ((0, 32),)),
        "linear_matrix": gaussian(seeds[13], (FF, D), D ** -0.5, 0.09375, ((0, 32),)),
        "down_matrix": draw_down_matrix(jax.random.fold_in(seeds[16], 71), 0),
        "closing_gain": jnp.clip(1.0 + 0.1 * jax.random.normal(seeds[15], (D,), jnp.float32), 0.5, 1.5).astype(jnp.bfloat16),
    }


norm_eps = 1e-06

def capped(scores):
    return SOFTCAP * jnp.tanh(scores / SOFTCAP)

def normalize(values, gain_row):
    mean_square = lax.optimization_barrier(jnp.mean(values * values, axis=1, keepdims=True))
    return values * lax.rsqrt(mean_square + norm_eps) * gain_row.astype(jnp.float32)[None, :]

def reference(queries, fresh_token_keys, fresh_token_values, paged_keys, paged_values, block_tables, parents, prompt_lengths, stream, output_matrix, attention_gain, feedforward_gain, gate_matrix, linear_matrix, down_matrix, closing_gain):
    query_groups = QUERY_HEADS // KEY_VALUE_HEADS
    root_scale = math.sqrt(QSCALAR)
    row_tables = jnp.take(block_tables, parents, axis=0)
    positions = jnp.arange(TABLE_BLOCKS * PAGE_TOKENS, dtype=jnp.int32)

    def one_row(current_row):
        fetched_pages = jnp.maximum(row_tables[current_row], 0)
        keys_of_row = jnp.take(paged_keys, fetched_pages, axis=0).reshape(TABLE_BLOCKS * PAGE_TOKENS, KEY_VALUE_HEADS, HEAD_DIM_SIZE).astype(jnp.float32)
        values_of_row = jnp.take(paged_values, fetched_pages, axis=0).reshape(TABLE_BLOCKS * PAGE_TOKENS, KEY_VALUE_HEADS, HEAD_DIM_SIZE).astype(jnp.float32)
        query_of_row = queries[current_row].reshape(KEY_VALUE_HEADS, query_groups, HEAD_DIM_SIZE).astype(jnp.float32)
        current_key = fresh_token_keys[current_row].reshape(KEY_VALUE_HEADS, HEAD_DIM_SIZE).astype(jnp.float32)
        current_value = fresh_token_values[current_row].reshape(KEY_VALUE_HEADS, HEAD_DIM_SIZE).astype(jnp.float32)
        limit = prompt_lengths[current_row // BEAMS]
        scores = capped(jnp.einsum('kgd,tkd->kgt', query_of_row, keys_of_row, precision=lax.Precision.HIGHEST) / root_scale)
        weights = jnp.where((positions < limit)[None, None, :], jnp.exp(scores), jnp.float32(0.0))
        self_weight = jnp.exp(capped(jnp.einsum('kgd,kd->kg', query_of_row, current_key, precision=lax.Precision.HIGHEST) / root_scale))
        totals = lax.optimization_barrier(jnp.sum(weights, axis=2)) + self_weight
        rounded = lax.optimization_barrier(weights.astype(jnp.bfloat16)).astype(jnp.float32)
        self_rounded = lax.optimization_barrier(self_weight.astype(jnp.bfloat16)).astype(jnp.float32)
        numerators = jnp.einsum('kgt,tkd->kgd', rounded, values_of_row, precision=lax.Precision.HIGHEST)
        numerators = numerators + self_rounded[:, :, None] * current_value[:, None, :]
        return (numerators / totals[:, :, None]).reshape(QUERY_HEADS * HEAD_DIM_SIZE).astype(jnp.bfloat16)
    attention = lax.map(one_row, jnp.arange(BEAM_ROW_COUNT, dtype=jnp.int32))
    projected = jnp.dot(attention, output_matrix.T, preferred_element_type=jnp.float32)
    residual = stream.astype(jnp.float32) + normalize(projected, attention_gain)
    normed = normalize(residual, feedforward_gain).astype(jnp.bfloat16)
    gate_sums = jnp.dot(normed, gate_matrix.T, preferred_element_type=jnp.float32)
    lift_sums = jnp.dot(normed, linear_matrix.T, preferred_element_type=jnp.float32)
    hidden = (jax.nn.gelu(gate_sums, approximate=True) * lift_sums).astype(jnp.bfloat16)
    feedforward = jnp.dot(hidden, down_matrix, preferred_element_type=jnp.float32)
    return (residual + normalize(feedforward, closing_gain)).astype(jnp.bfloat16)
```

```python
import functools
import math

import jax
import jax.numpy as jnp
from jax import lax
from jax.experimental import pallas as pl
from jax.experimental.pallas import tpu as pltpu
from jax.sharding import PartitionSpec as P

HEAD = 128
QSCALAR = 144
SOFTCAP = 50
BEAMS = 8
EPS = 1e-06

F32 = jnp.float32
BF16 = jnp.bfloat16
MESH = pl.DeviceIdType.MESH
NT = (((1,), (1,)), ((), ()))
NN = (((1,), (0,)), ((), ()))


def capped_exp(raw):
    return jnp.exp(SOFTCAP * jnp.tanh(raw * (1.0 / (math.sqrt(QSCALAR) * SOFTCAP))))


def mm(a, b, dims):
    return lax.dot_general(a, b, dims, preferred_element_type=F32)


def layer_kernel(
    n_page, n_feat, width, depth,
    q_ref, fk_ref, fv_ref, by_col_ref, by_row_ref, stream_ref, gains_ref,
    keys_hbm, values_hbm, wo_hbm, gate_hbm, lift_hbm, down_hbm,
    out_ref,
    kbuf, vbuf, wo, gate, lift, down,
    allq, qs, nvs, snum, stot, nsend, nrecv, att, strm, prj, res,
    xg, xs, gacc, uacc, hid, core_s, core_r, y_s, y_r, psend, precv, fsend, frecv,
    kv_sem, w_sem,
    q_ss, q_rs, n_ss, n_rs, st_ss, st_rs, pj_ss, pj_rs, ag_ss, ag_rs,
    xy_ss, xc_ss, x_rs, c_ss, c_rs, y_ss, y_rs, p_ss, p_rs, f_ss, f_rs,
):
    page = lax.axis_index("page")
    feat = lax.axis_index("feat")
    ny = n_feat // 2
    yy, cc = feat // 2, feat % 2
    mate = yy * 2 + (1 - cc)
    slots, page_len, kvw = kbuf.shape
    kv_heads = kvw // HEAD
    heads = q_ref.shape[1] // HEAD
    groups = heads // kv_heads
    rows = n_page * BEAMS
    home = stream_ref.shape[0]
    hw = heads * HEAD

    def cut(c):
        return min(width, depth - c * width)

    local = [
        pltpu.make_async_copy(keys_hbm, kbuf, kv_sem.at[0]),
        pltpu.make_async_copy(values_hbm, vbuf, kv_sem.at[1]),
    ]
    w_copies = [[], [], [], []]
    for c in range(n_feat):
        part = pl.ds(c * width, cut(c))
        have = pl.ds(0, cut(c))
        w_copies[0].append(pltpu.make_async_copy(wo_hbm.at[part, :], wo.at[c, have, :], w_sem.at[0, c]))
        w_copies[1].append(pltpu.make_async_copy(gate_hbm.at[:, part], gate.at[c, :, have], w_sem.at[1, c]))
        w_copies[2].append(pltpu.make_async_copy(lift_hbm.at[:, part], lift.at[c, :, have], w_sem.at[2, c]))
        w_copies[3].append(pltpu.make_async_copy(down_hbm.at[:, part], down.at[c, :, have], w_sem.at[3, c]))
        if cut(c) < width:
            rest = width - cut(c)
            wo[c, cut(c):, :] = jnp.zeros((rest, wo.shape[2]), BF16)
            gate[c, :, cut(c):] = jnp.zeros((gate.shape[1], rest), BF16)
            lift[c, :, cut(c):] = jnp.zeros((gate.shape[1], rest), BF16)
            down[c, :, cut(c):] = jnp.zeros((gate.shape[1], rest), BF16)
    for copy in local:
        copy.start()
    for kind in w_copies:
        for copy in kind:
            copy.start()

    barrier = pltpu.get_barrier_semaphore()

    def greet_page(d, _):
        pl.semaphore_signal(barrier, inc=1, device_id=((page + d) % n_page, feat), device_id_type=MESH)
        return 0

    def greet_feat(d, _):
        pl.semaphore_signal(barrier, inc=1, device_id=(page, (feat + d) % n_feat), device_id_type=MESH)
        return 0

    lax.fori_loop(1, n_page, greet_page, 0)
    lax.fori_loop(1, n_feat, greet_feat, 0)

    allq[page] = q_ref[...]
    sf = stream_ref[...].astype(F32)
    if strm.shape[2] > depth:
        sf = jnp.concatenate([sf, jnp.zeros((home, strm.shape[2] - depth), F32)], axis=1)
    strm[feat] = sf
    pl.semaphore_wait(barrier, n_page + n_feat - 2)

    def page_copy(src, dst, ss, rs):
        def send(d):
            peer = (page + d) % n_page
            return pltpu.make_async_remote_copy(
                src_ref=src(peer), dst_ref=dst(page), send_sem=ss.at[peer], recv_sem=rs.at[page],
                device_id=(peer, feat), device_id_type=MESH)

        def arrival(d):
            peer = (page + d) % n_page
            return pltpu.make_async_remote_copy(
                src_ref=src(peer), dst_ref=dst(peer), send_sem=ss.at[peer], recv_sem=rs.at[peer],
                device_id=(peer, feat), device_id_type=MESH)

        def start():
            lax.fori_loop(1, n_page, lambda d, z: (send(d).start(), z)[1], 0)

        def wait_recv():
            lax.fori_loop(1, n_page, lambda d, z: (arrival(d).wait_recv(), z)[1], 0)

        def wait_send():
            lax.fori_loop(1, n_page, lambda d, z: (send(d).wait_send(), z)[1], 0)

        return start, wait_recv, wait_send

    def feat_copy(src, dst, ss, rs):
        def send(d):
            peer = (feat + d) % n_feat
            return pltpu.make_async_remote_copy(
                src_ref=src(peer), dst_ref=dst(feat), send_sem=ss(peer), recv_sem=rs(feat),
                device_id=(page, peer), device_id_type=MESH)

        def arrival(d):
            peer = (feat + d) % n_feat
            return pltpu.make_async_remote_copy(
                src_ref=src(peer), dst_ref=dst(peer), send_sem=ss(peer), recv_sem=rs(peer),
                device_id=(page, peer), device_id_type=MESH)

        def start():
            lax.fori_loop(1, n_feat, lambda d, z: (send(d).start(), z)[1], 0)

        def wait_recv():
            lax.fori_loop(1, n_feat, lambda d, z: (arrival(d).wait_recv(), z)[1], 0)

        def wait_send():
            lax.fori_loop(1, n_feat, lambda d, z: (send(d).wait_send(), z)[1], 0)

        return start, wait_recv, wait_send

    q_start, q_wait, q_done = page_copy(lambda p: allq.at[page], lambda p: allq.at[p], q_ss, q_rs)
    q_start()
    st_start, st_wait, st_done = feat_copy(
        lambda p: strm.at[feat], lambda p: strm.at[p], lambda p: st_ss.at[p], lambda p: st_rs.at[p])
    st_start()

    blocks = by_col_ref.shape[0] - 1
    sb = slots * BEAMS
    down_i = lax.broadcasted_iota(jnp.int32, (sb, rows), 0)
    across = lax.broadcasted_iota(jnp.int32, (sb, rows), 1)
    seen = jnp.zeros((sb, rows), jnp.int32)
    lens = by_col_ref[blocks:blocks + 1, :]
    for b in range(blocks):
        seen += jnp.where(by_col_ref[b:b + 1, :] == page * slots + down_i // BEAMS,
                          jnp.clip(lens - b * page_len, 0, page_len), 0)
    seen = jnp.where(across % BEAMS == down_i % BEAMS, seen, 0).astype(F32)
    pick = jnp.where(seen > 0, 1.0, 0.0).astype(BF16)
    nvs[...] = jnp.broadcast_to(jnp.sum(seen, axis=1, keepdims=True), nvs.shape)

    down_t = lax.broadcasted_iota(jnp.int32, (rows, sb), 0)
    across_t = lax.broadcasted_iota(jnp.int32, (rows, sb), 1)
    seen_t = jnp.zeros((rows, sb), jnp.int32)
    lens_t = by_row_ref[:, blocks:blocks + 1]
    for b in range(blocks):
        seen_t += jnp.where(by_row_ref[:, b:b + 1] == page * slots + across_t // BEAMS,
                            jnp.clip(lens_t - b * page_len, 0, page_len), 0)
    pick_t = jnp.where(jnp.logical_and(across_t % BEAMS == down_t % BEAMS, seen_t > 0), 1.0, 0.0).astype(BF16)

    q_wait()
    q_all = allq[...].astype(F32).reshape(rows, hw).astype(BF16)
    qs[...] = mm(pick, q_all, NN)
    for copy in local:
        copy.wait()

    lane = lax.broadcasted_iota(jnp.int32, (BEAMS, HEAD), 1)
    position = lax.broadcasted_iota(jnp.int32, (groups * BEAMS, page_len), 1).astype(F32)

    def one_slot(s):
        at = pl.ds(pl.multiple_of(s * BEAMS, BEAMS), BEAMS)
        limit = jnp.concatenate([nvs[at, :]] * groups, axis=0)[:, 0:1]
        visible = position < limit
        sums = jnp.zeros((BEAMS, HEAD), F32)
        for k in range(kv_heads):
            kv = slice(k * HEAD, (k + 1) * HEAD)
            qk = jnp.concatenate(
                [qs[at, (k * groups + g) * HEAD:(k * groups + g + 1) * HEAD] for g in range(groups)], axis=0)
            raw = mm(qk.astype(BF16), kbuf[s, :, kv], NT)
            w = jnp.where(visible, capped_exp(raw), 0.0)
            tot = jnp.sum(w, axis=1, keepdims=True)
            num = mm(w.astype(BF16), vbuf[s, :, kv], NN)
            for g in range(groups):
                h = k * groups + g
                snum[at, h * HEAD:(h + 1) * HEAD] = num[g * BEAMS:(g + 1) * BEAMS]
                sums = jnp.where(lane == h, tot[g * BEAMS:(g + 1) * BEAMS], sums)
        stot[at, :] = sums

    per = 2 if slots % 2 == 0 else 1

    def some_slots(i, z):
        for u in range(per):
            one_slot(i * per + u)
        return z

    lax.fori_loop(0, slots // per, some_slots, 0)

    def to_rows(v):
        hi = v.astype(BF16)
        lo = (v - hi.astype(F32)).astype(BF16)
        return mm(pick_t, hi, NN) + mm(pick_t, lo, NN)

    tot_rows = to_rows(stot[...])
    tot_hi = tot_rows.astype(BF16)
    tot_lo = tot_rows - tot_hi.astype(F32)
    nsend[:, :, 0:hw] = to_rows(snum[...]).reshape(n_page, BEAMS, hw).astype(BF16)
    nsend[:, :, hw:hw + HEAD] = tot_hi.astype(F32).reshape(n_page, BEAMS, HEAD).astype(BF16)
    nsend[:, :, hw + HEAD:hw + 2 * HEAD] = tot_lo.reshape(n_page, BEAMS, HEAD).astype(BF16)
    nrecv[page] = nsend[page]
    n_start, n_wait, n_done = page_copy(lambda p: nsend.at[p], lambda p: nrecv.at[p], n_ss, n_rs)
    n_start()

    own_w = []
    for h in range(heads):
        k = h // groups
        qk = q_ref[:, h * HEAD:(h + 1) * HEAD].astype(F32) * fk_ref[:, k * HEAD:(k + 1) * HEAD].astype(F32)
        own_w.append(capped_exp(jnp.sum(qk, axis=1, keepdims=True)))
    n_wait()
    totals = jnp.sum(nrecv[:, :, hw:hw + HEAD].astype(F32) + nrecv[:, :, hw + HEAD:hw + 2 * HEAD].astype(F32), axis=0)
    for h in range(heads):
        k = h // groups
        hs = slice(h * HEAD, (h + 1) * HEAD)
        num = jnp.sum(nrecv[:, :, hs].astype(F32), axis=0)
        num += own_w[h].astype(BF16).astype(F32) * fv_ref[:, k * HEAD:(k + 1) * HEAD].astype(F32)
        att[:, hs] = (num / (totals[:, h:h + 1] + own_w[h])).astype(BF16)

    for copy in w_copies[0]:
        copy.wait()

    def pj(c):
        return feat_copy(lambda p: prj.at[feat, c], lambda p: prj.at[p, c],
                         lambda p: pj_ss.at[p, c], lambda p: pj_rs.at[p, c])

    def project(c, z):
        prj[feat, c] = mm(att[...], wo[c], NT).astype(BF16)
        pj(c)[0]()
        return z

    lax.fori_loop(0, n_feat, project, 0)
    st_wait()
    lax.fori_loop(0, n_feat, lambda c, z: (pj(c)[1](), z)[1], 0)

    square = jnp.zeros((BEAMS, 1), F32)
    for c in range(n_feat):
        v = jnp.sum(prj[:, c].astype(F32), axis=0)
        res[c] = v
        square += jnp.sum(v * v, axis=1, keepdims=True)
    scale = lax.rsqrt(square / depth + EPS)
    square = jnp.zeros((BEAMS, 1), F32)
    for c in range(n_feat):
        cols = slice(c * width, (c + 1) * width)
        base = jnp.concatenate([strm[g, :, cols] for g in range(n_feat)], axis=0)
        v = base + res[c] * scale * gains_ref[0, c]
        res[c] = v
        square += jnp.sum(v * v, axis=1, keepdims=True)
    scale = lax.rsqrt(square / depth + EPS)
    xg[feat, page] = (res[feat] * scale * gains_ref[1, feat]).astype(BF16)

    ag_start, ag_wait, ag_done = page_copy(
        lambda p: xg.at[feat, page], lambda p: xg.at[feat, p], ag_ss, ag_rs)
    ag_start()
    for kind in w_copies[1:3]:
        for copy in kind:
            copy.wait()

    def chunk_copy(q, peer, ss):
        return pltpu.make_async_remote_copy(
            src_ref=xg.at[q], dst_ref=xg.at[q], send_sem=ss, recv_sem=x_rs.at[q],
            device_id=(page, peer), device_id_type=MESH)

    ag_wait()
    sends = []
    for d in range(1, ny):
        sends.append(chunk_copy(feat, ((yy + d) % ny) * 2 + cc, xy_ss.at[d]))
        sends[-1].start()
    sends.append(chunk_copy(feat, mate, xc_ss.at[0]))
    sends[-1].start()
    for d in range(ny):
        for o in range(2):
            q = ((yy + ny - d) % ny) * 2 + (cc if o == 0 else 1 - cc)
            if d or o:
                chunk_copy(q, mate, xc_ss.at[d]).wait_recv()
            if d and not o:
                sends.append(chunk_copy(q, mate, xc_ss.at[d]))
                sends[-1].start()
            xs[...] = xg[q].astype(F32).reshape(rows, width).astype(BF16)
            if d or o:
                gacc[...] += mm(xs[...], gate[q], NT)
                uacc[...] += mm(xs[...], lift[q], NT)
            else:
                gacc[...] = mm(xs[...], gate[q], NT)
                uacc[...] = mm(xs[...], lift[q], NT)
    hid[...] = (jax.nn.gelu(gacc[...], approximate=True) * uacc[...]).astype(BF16)

    for copy in w_copies[3]:
        copy.wait()
    total = None
    for d in list(range(1, ny)) + [0]:
        yq = (yy + d) % ny
        core_s[d] = mm(hid[...], down[yq * 2 + (1 - cc)], NN).astype(BF16)
        over = pltpu.make_async_remote_copy(
            src_ref=core_s.at[d], dst_ref=core_r.at[d], send_sem=c_ss.at[d], recv_sem=c_rs.at[d],
            device_id=(page, mate), device_id_type=MESH)
        over.start()
        sends.append(over)
        part = mm(hid[...], down[yq * 2 + cc], NN)
        over.wait_recv()
        part = part + core_r[d].astype(F32)
        if d:
            y_s[d - 1] = part.astype(BF16)
            along = pltpu.make_async_remote_copy(
                src_ref=y_s.at[d - 1], dst_ref=y_r.at[d - 1], send_sem=y_ss.at[d - 1], recv_sem=y_rs.at[d - 1],
                device_id=(page, yq * 2 + cc), device_id_type=MESH)
            along.start()
            sends.append(along)
        else:
            total = part
    for d in range(1, ny):
        pltpu.make_async_remote_copy(
            src_ref=y_s.at[d - 1], dst_ref=y_r.at[d - 1], send_sem=y_ss.at[d - 1], recv_sem=y_rs.at[d - 1],
            device_id=(page, mate), device_id_type=MESH).wait_recv()
        total = total + y_r[d - 1].astype(F32)
    psend[...] = total.reshape(n_page, BEAMS, width).astype(BF16)
    precv[page] = psend[page]
    p_start, p_wait, p_done = page_copy(lambda p: psend.at[p], lambda p: precv.at[p], p_ss, p_rs)
    p_start()
    p_wait()
    ff = jnp.sum(precv[...].astype(F32), axis=0)
    for g in range(n_feat):
        fsend[g] = ff[g * home:(g + 1) * home]
    frecv[feat] = fsend[feat]
    f_start, f_wait, f_done = feat_copy(
        lambda p: fsend.at[p], lambda p: frecv.at[p], lambda p: f_ss.at[p], lambda p: f_rs.at[p])
    f_start()
    f_wait()
    square = jnp.zeros((home, 1), F32)
    for c in range(n_feat):
        v = frecv[c]
        square += jnp.sum(v * v, axis=1, keepdims=True)
    scale = lax.rsqrt(square / depth + EPS)
    for c in range(n_feat):
        base = jnp.zeros((home, width), F32)
        r8 = res[c]
        for g in range(n_feat):
            base = jnp.where(feat == g, r8[g * home:(g + 1) * home], base)
        v = base + frecv[c] * scale * gains_ref[2, c]
        out_ref[:, c * width:c * width + cut(c)] = v[:, 0:cut(c)].astype(BF16)

    q_done()
    st_done()
    n_done()
    lax.fori_loop(0, n_feat, lambda c, z: (pj(c)[2](), z)[1], 0)
    ag_done()
    for copy in sends:
        copy.wait_send()
    p_done()
    f_done()


def per_device(
    n_page, n_feat,
    queries, fresh_keys, fresh_values, paged_keys, paged_values, block_tables, parents, prompt_lengths,
    stream, output_matrix, attention_gain, feedforward_gain, gate_matrix, linear_matrix, down_matrix, closing_gain,
):
    depth = stream.shape[1]
    home = stream.shape[0]
    tiles = -(-depth // 128)
    width = -(-tiles // n_feat) * 128
    padded = width * n_feat
    rows = n_page * queries.shape[0]
    slots, page_len, kvw = paged_keys.shape
    hw = queries.shape[1]
    units = gate_matrix.shape[0]
    ny = n_feat // 2
    sb = slots * BEAMS

    tables = jnp.concatenate([block_tables, jnp.repeat(prompt_lengths, BEAMS)[:, None]], axis=1)
    chosen = parents[:, None] == jnp.arange(rows, dtype=jnp.int32)[None, :]
    by_row = jnp.sum(jnp.where(chosen[:, :, None], tables[None, :, :], 0), axis=1)
    by_col = jnp.sum(jnp.where(chosen.T[:, None, :], tables[:, :, None], 0), axis=0)
    gains = jnp.stack([attention_gain, feedforward_gain, closing_gain]).astype(F32)
    gains = jnp.pad(gains, ((0, 0), (0, padded - depth))).reshape(3, n_feat, 1, width)

    dma = pltpu.SemaphoreType.DMA
    scratch = [
        pltpu.VMEM(paged_keys.shape, BF16), pltpu.VMEM(paged_values.shape, BF16),
        pltpu.VMEM((n_feat, width, hw), BF16),
        pltpu.VMEM((n_feat, units, width), BF16), pltpu.VMEM((n_feat, units, width), BF16),
        pltpu.VMEM((n_feat, units, width), BF16),
        pltpu.VMEM((n_page, BEAMS, hw), BF16),
        pltpu.VMEM((sb, hw), F32),
        pltpu.VMEM((sb, HEAD), F32),
        pltpu.VMEM((sb, hw), F32),
        pltpu.VMEM((sb, HEAD), F32),
        pltpu.VMEM((n_page, BEAMS, hw + 2 * HEAD), BF16),
        pltpu.VMEM((n_page, BEAMS, hw + 2 * HEAD), BF16),
        pltpu.VMEM((BEAMS, hw), BF16),
        pltpu.VMEM((n_feat, home, padded), F32),
        pltpu.VMEM((n_feat, n_feat, BEAMS, width), BF16),
        pltpu.VMEM((n_feat, BEAMS, width), F32),
        pltpu.VMEM((n_feat, n_page, BEAMS, width), BF16),
        pltpu.VMEM((rows, width), BF16),
        pltpu.VMEM((rows, units), F32), pltpu.VMEM((rows, units), F32),
        pltpu.VMEM((rows, units), BF16),
        pltpu.VMEM((ny, rows, width), BF16), pltpu.VMEM((ny, rows, width), BF16),
        pltpu.VMEM((ny - 1, rows, width), BF16), pltpu.VMEM((ny - 1, rows, width), BF16),
        pltpu.VMEM((n_page, BEAMS, width), BF16), pltpu.VMEM((n_page, BEAMS, width), BF16),
        pltpu.VMEM((n_feat, home, width), F32), pltpu.VMEM((n_feat, home, width), F32),
        dma((2,)), dma((4, n_feat)),
        dma((n_page,)), dma((n_page,)),
        dma((n_page,)), dma((n_page,)),
        dma((n_feat,)), dma((n_feat,)),
        dma((n_feat, n_feat)), dma((n_feat, n_feat)),
        dma((n_page,)), dma((n_page,)),
        dma((ny,)), dma((ny,)), dma((n_feat,)),
        dma((ny,)), dma((ny,)), dma((ny - 1,)), dma((ny - 1,)),
        dma((n_page,)), dma((n_page,)),
        dma((n_feat,)), dma((n_feat,)),
    ]
    vmem = pl.BlockSpec(memory_space=pltpu.VMEM)
    hbm = pl.BlockSpec(memory_space=pl.ANY)
    return pl.pallas_call(
        functools.partial(layer_kernel, n_page, n_feat, width, depth),
        out_shape=jax.ShapeDtypeStruct((home, depth), BF16),
        in_specs=[vmem] * 7 + [hbm] * 6,
        out_specs=vmem,
        scratch_shapes=scratch,
        compiler_params=pltpu.CompilerParams(
            collective_id=0, has_side_effects=True, vmem_limit_bytes=60 * 2**20),
    )(queries, fresh_keys, fresh_values, by_col, by_row, stream, gains,
      paged_keys, paged_values, output_matrix, gate_matrix, linear_matrix, down_matrix)


def solution(mesh):
    both = P(("page", "feat"), None)
    placed = (
        P("page", "feat"), P("page", "feat"), P("page", "feat"),
        P("page", None, "feat"), P("page", None, "feat"),
        P(), P(), P(), both, P(None, "feat"), P(), P(), both, both, both, P(),
    )
    return jax.shard_map(
        functools.partial(per_device, mesh.shape["page"], mesh.shape["feat"]),
        mesh=mesh, in_specs=placed, out_specs=both, check_vma=False)
```

```python
import functools
import math

import jax
import jax.numpy as jnp
from jax import lax
from jax.experimental import pallas as pl
from jax.experimental.pallas import tpu as pltpu
from jax.sharding import PartitionSpec as P

HEAD = 128
QSCALAR = 144
SOFTCAP = 50
BEAMS = 8
EPS = 1e-06

F32 = jnp.float32
BF16 = jnp.bfloat16
MESH = pl.DeviceIdType.MESH
NT = (((1,), (1,)), ((), ()))
NN = (((1,), (0,)), ((), ()))
TN = (((0,), (0,)), ((), ()))


def capped_exp(raw):
    return jnp.exp(SOFTCAP * jnp.tanh(raw * (1.0 / (math.sqrt(QSCALAR) * SOFTCAP))))


def mm(a, b, dims):
    return lax.dot_general(a, b, dims, preferred_element_type=F32)


def layer_kernel(
    n_page, n_feat, width, depth,
    q_ref, fk_ref, fv_ref, tables_ref, parents_ref, lengths_ref, stream_ref, gains_ref,
    keys_hbm, values_hbm, wo_hbm, gate_hbm, lift_hbm, down_hbm,
    out_ref,
    kbuf, vbuf, wo, gate, lift, down,
    by_row, row_lens, allq, qs, nvs, snum, stot, nsend, nrecv, att, strm, prj, res,
    xg, xs, gacc, uacc, hid, core_s, core_r, y_s, y_r, psend, precv, fsend, frecv,
    kv_sem, w_sem,
    q_ss, q_rs, n_ss, n_rs, st_ss, st_rs, pj_ss, pj_rs, ag_ss, ag_rs,
    xy_ss, xc_ss, x_rs, c_ss, c_rs, y_ss, y_rs, p_ss, p_rs, f_ss, f_rs,
):
    page = lax.axis_index("page")
    feat = lax.axis_index("feat")
    ny = n_feat // 2
    yy, cc = feat // 2, feat % 2
    mate = yy * 2 + (1 - cc)
    slots, page_len, kvw = kbuf.shape
    kv_heads = kvw // HEAD
    heads = q_ref.shape[1] // HEAD
    groups = heads // kv_heads
    rows = n_page * BEAMS
    home = stream_ref.shape[0]
    hw = heads * HEAD

    def cut(c):
        return min(width, depth - c * width)

    local = [
        pltpu.make_async_copy(keys_hbm, kbuf, kv_sem.at[0]),
        pltpu.make_async_copy(values_hbm, vbuf, kv_sem.at[1]),
    ]
    w_copies = [[], [], [], []]
    for c in range(n_feat):
        part = pl.ds(c * width, cut(c))
        have = pl.ds(0, cut(c))
        w_copies[0].append(pltpu.make_async_copy(wo_hbm.at[part, :], wo.at[c, have, :], w_sem.at[0, c]))
        w_copies[1].append(pltpu.make_async_copy(gate_hbm.at[:, part], gate.at[c, :, have], w_sem.at[1, c]))
        w_copies[2].append(pltpu.make_async_copy(lift_hbm.at[:, part], lift.at[c, :, have], w_sem.at[2, c]))
        w_copies[3].append(pltpu.make_async_copy(down_hbm.at[:, part], down.at[c, :, have], w_sem.at[3, c]))
        if cut(c) < width:
            rest = width - cut(c)
            wo[c, cut(c):, :] = jnp.zeros((rest, wo.shape[2]), BF16)
            gate[c, :, cut(c):] = jnp.zeros((gate.shape[1], rest), BF16)
            lift[c, :, cut(c):] = jnp.zeros((gate.shape[1], rest), BF16)
            down[c, :, cut(c):] = jnp.zeros((gate.shape[1], rest), BF16)
    for copy in local:
        copy.start()

    barrier = pltpu.get_barrier_semaphore()

    def greet_page(d, _):
        pl.semaphore_signal(barrier, inc=1, device_id=((page + d) % n_page, feat), device_id_type=MESH)
        return 0

    def greet_feat(d, _):
        pl.semaphore_signal(barrier, inc=1, device_id=(page, (feat + d) % n_feat), device_id_type=MESH)
        return 0

    lax.fori_loop(1, n_page, greet_page, 0)
    lax.fori_loop(1, n_feat, greet_feat, 0)

    allq[page] = q_ref[...]
    sf = stream_ref[...].astype(F32)
    if strm.shape[2] > depth:
        sf = jnp.concatenate([sf, jnp.zeros((home, strm.shape[2] - depth), F32)], axis=1)
    strm[feat] = sf
    pl.semaphore_wait(barrier, n_page + n_feat - 2)

    def page_copy(src, dst, ss, rs):
        def send(d):
            peer = (page + d) % n_page
            return pltpu.make_async_remote_copy(
                src_ref=src(peer), dst_ref=dst(page), send_sem=ss.at[peer], recv_sem=rs.at[page],
                device_id=(peer, feat), device_id_type=MESH)

        def arrival(d):
            peer = (page + d) % n_page
            return pltpu.make_async_remote_copy(
                src_ref=src(peer), dst_ref=dst(peer), send_sem=ss.at[peer], recv_sem=rs.at[peer],
                device_id=(peer, feat), device_id_type=MESH)

        def start():
            lax.fori_loop(1, n_page, lambda d, z: (send(d).start(), z)[1], 0)

        def wait_recv():
            lax.fori_loop(1, n_page, lambda d, z: (arrival(d).wait_recv(), z)[1], 0)

        def wait_send():
            lax.fori_loop(1, n_page, lambda d, z: (send(d).wait_send(), z)[1], 0)

        return start, wait_recv, wait_send

    def feat_copy(src, dst, ss, rs):
        def send(d):
            peer = (feat + d) % n_feat
            return pltpu.make_async_remote_copy(
                src_ref=src(peer), dst_ref=dst(feat), send_sem=ss(peer), recv_sem=rs(feat),
                device_id=(page, peer), device_id_type=MESH)

        def arrival(d):
            peer = (feat + d) % n_feat
            return pltpu.make_async_remote_copy(
                src_ref=src(peer), dst_ref=dst(peer), send_sem=ss(peer), recv_sem=rs(peer),
                device_id=(page, peer), device_id_type=MESH)

        def start():
            lax.fori_loop(1, n_feat, lambda d, z: (send(d).start(), z)[1], 0)

        def wait_recv():
            lax.fori_loop(1, n_feat, lambda d, z: (arrival(d).wait_recv(), z)[1], 0)

        def wait_send():
            lax.fori_loop(1, n_feat, lambda d, z: (send(d).wait_send(), z)[1], 0)

        return start, wait_recv, wait_send

    q_start, q_wait, q_done = page_copy(lambda p: allq.at[page], lambda p: allq.at[p], q_ss, q_rs)
    q_start()
    st_start, st_wait, st_done = feat_copy(
        lambda p: strm.at[feat], lambda p: strm.at[p], lambda p: st_ss.at[p], lambda p: st_rs.at[p])
    st_start()

    def one_row(r, z):
        by_row[pl.ds(r, 1), :] = tables_ref[pl.ds(parents_ref[r], 1), :]
        row_lens[pl.ds(r, 1), :] = jnp.full((1, HEAD), lengths_ref[r // BEAMS], jnp.int32)
        return z

    lax.fori_loop(0, rows, one_row, 0, unroll=8)
    blocks = tables_ref.shape[1]
    sb = slots * BEAMS
    row_i = lax.broadcasted_iota(jnp.int32, (rows, sb), 0)
    spot_i = lax.broadcasted_iota(jnp.int32, (rows, sb), 1)
    lens = row_lens[:, 0:1]
    seen = jnp.zeros((rows, sb), jnp.int32)
    for b in range(blocks):
        seen += jnp.where(by_row[:, b:b + 1] == page * slots + spot_i // BEAMS,
                          jnp.clip(lens - b * page_len, 0, page_len), 0)
    seen = jnp.where(spot_i % BEAMS == row_i % BEAMS, seen, 0).astype(F32)
    pick_t = jnp.where(seen > 0, 1.0, 0.0).astype(BF16)
    nvs[...] = mm(seen.astype(BF16), jnp.ones((rows, HEAD), BF16), TN)

    q_wait()
    q_all = allq[...].astype(F32).reshape(rows, hw).astype(BF16)
    qs[...] = mm(pick_t, q_all, TN)
    for copy in local:
        copy.wait()
    for kind in w_copies:
        for copy in kind:
            copy.start()

    lane = lax.broadcasted_iota(jnp.int32, (BEAMS, HEAD), 1)
    position = lax.broadcasted_iota(jnp.int32, (groups * BEAMS, page_len), 1).astype(F32)

    def one_slot(s):
        at = pl.ds(pl.multiple_of(s * BEAMS, BEAMS), BEAMS)
        limit = jnp.concatenate([nvs[at, :]] * groups, axis=0)[:, 0:1]
        visible = position < limit
        sums = jnp.zeros((BEAMS, HEAD), F32)
        for k in range(kv_heads):
            kv = slice(k * HEAD, (k + 1) * HEAD)
            qk = jnp.concatenate(
                [qs[at, (k * groups + g) * HEAD:(k * groups + g + 1) * HEAD] for g in range(groups)], axis=0)
            raw = mm(qk.astype(BF16), kbuf[s, :, kv], NT)
            w = jnp.where(visible, capped_exp(raw), 0.0)
            tot = jnp.sum(w, axis=1, keepdims=True)
            num = mm(w.astype(BF16), vbuf[s, :, kv], NN)
            for g in range(groups):
                h = k * groups + g
                snum[at, h * HEAD:(h + 1) * HEAD] = num[g * BEAMS:(g + 1) * BEAMS]
                sums = jnp.where(lane == h, tot[g * BEAMS:(g + 1) * BEAMS], sums)
        stot[at, :] = sums

    per = 2 if slots % 2 == 0 else 1

    def some_slots(i, z):
        for u in range(per):
            one_slot(i * per + u)
        return z

    lax.fori_loop(0, slots // per, some_slots, 0)

    def to_rows(v):
        hi = v.astype(BF16)
        lo = (v - hi.astype(F32)).astype(BF16)
        return mm(pick_t, hi, NN) + mm(pick_t, lo, NN)

    tot_rows = to_rows(stot[...])
    tot_hi = tot_rows.astype(BF16)
    tot_lo = tot_rows - tot_hi.astype(F32)
    nsend[:, :, 0:hw] = to_rows(snum[...]).reshape(n_page, BEAMS, hw).astype(BF16)
    nsend[:, :, hw:hw + HEAD] = tot_hi.astype(F32).reshape(n_page, BEAMS, HEAD).astype(BF16)
    nsend[:, :, hw + HEAD:hw + 2 * HEAD] = tot_lo.reshape(n_page, BEAMS, HEAD).astype(BF16)
    nrecv[page] = nsend[page]
    n_start, n_wait, n_done = page_copy(lambda p: nsend.at[p], lambda p: nrecv.at[p], n_ss, n_rs)
    n_start()

    own_w = []
    for h in range(heads):
        k = h // groups
        qk = q_ref[:, h * HEAD:(h + 1) * HEAD].astype(F32) * fk_ref[:, k * HEAD:(k + 1) * HEAD].astype(F32)
        own_w.append(capped_exp(jnp.sum(qk, axis=1, keepdims=True)))
    n_wait()
    totals = jnp.sum(nrecv[:, :, hw:hw + HEAD].astype(F32) + nrecv[:, :, hw + HEAD:hw + 2 * HEAD].astype(F32), axis=0)
    for h in range(heads):
        k = h // groups
        hs = slice(h * HEAD, (h + 1) * HEAD)
        num = jnp.sum(nrecv[:, :, hs].astype(F32), axis=0)
        num += own_w[h].astype(BF16).astype(F32) * fv_ref[:, k * HEAD:(k + 1) * HEAD].astype(F32)
        att[:, hs] = (num / (totals[:, h:h + 1] + own_w[h])).astype(BF16)

    for copy in w_copies[0]:
        copy.wait()

    def pj(c):
        return feat_copy(lambda p: prj.at[feat, c], lambda p: prj.at[p, c],
                         lambda p: pj_ss.at[p, c], lambda p: pj_rs.at[p, c])

    def project(c, z):
        prj[feat, c] = mm(att[...], wo[c], NT).astype(BF16)
        pj(c)[0]()
        return z

    lax.fori_loop(0, n_feat, project, 0)
    st_wait()
    lax.fori_loop(0, n_feat, lambda c, z: (pj(c)[1](), z)[1], 0)

    square = jnp.zeros((BEAMS, 1), F32)
    for c in range(n_feat):
        v = jnp.sum(prj[:, c].astype(F32), axis=0)
        res[c] = v
        square += jnp.sum(v * v, axis=1, keepdims=True)
    scale = lax.rsqrt(square / depth + EPS)
    square = jnp.zeros((BEAMS, 1), F32)
    for c in range(n_feat):
        cols = slice(c * width, (c + 1) * width)
        base = jnp.concatenate([strm[g, :, cols] for g in range(n_feat)], axis=0)
        v = base + res[c] * scale * gains_ref[0, c]
        res[c] = v
        square += jnp.sum(v * v, axis=1, keepdims=True)
    scale = lax.rsqrt(square / depth + EPS)
    xg[feat, page] = (res[feat] * scale * gains_ref[1, feat]).astype(BF16)

    ag_start, ag_wait, ag_done = page_copy(
        lambda p: xg.at[feat, page], lambda p: xg.at[feat, p], ag_ss, ag_rs)
    ag_start()
    for kind in w_copies[1:3]:
        for copy in kind:
            copy.wait()

    def chunk_copy(q, peer, ss):
        return pltpu.make_async_remote_copy(
            src_ref=xg.at[q], dst_ref=xg.at[q], send_sem=ss, recv_sem=x_rs.at[q],
            device_id=(page, peer), device_id_type=MESH)

    ag_wait()
    sends = []
    for d in range(1, ny):
        sends.append(chunk_copy(feat, ((yy + d) % ny) * 2 + cc, xy_ss.at[d]))
        sends[-1].start()
    sends.append(chunk_copy(feat, mate, xc_ss.at[0]))
    sends[-1].start()
    for d in range(ny):
        for o in range(2):
            q = ((yy + ny - d) % ny) * 2 + (cc if o == 0 else 1 - cc)
            if d or o:
                chunk_copy(q, mate, xc_ss.at[d]).wait_recv()
            if d and not o:
                sends.append(chunk_copy(q, mate, xc_ss.at[d]))
                sends[-1].start()
            xs[...] = xg[q].astype(F32).reshape(rows, width).astype(BF16)
            if d or o:
                gacc[...] += mm(xs[...], gate[q], NT)
                uacc[...] += mm(xs[...], lift[q], NT)
            else:
                gacc[...] = mm(xs[...], gate[q], NT)
                uacc[...] = mm(xs[...], lift[q], NT)
    hid[...] = (jax.nn.gelu(gacc[...], approximate=True) * uacc[...]).astype(BF16)

    for copy in w_copies[3]:
        copy.wait()
    total = None
    for d in list(range(1, ny)) + [0]:
        yq = (yy + d) % ny
        core_s[d] = mm(hid[...], down[yq * 2 + (1 - cc)], NN).astype(BF16)
        over = pltpu.make_async_remote_copy(
            src_ref=core_s.at[d], dst_ref=core_r.at[d], send_sem=c_ss.at[d], recv_sem=c_rs.at[d],
            device_id=(page, mate), device_id_type=MESH)
        over.start()
        sends.append(over)
        part = mm(hid[...], down[yq * 2 + cc], NN)
        over.wait_recv()
        part = part + core_r[d].astype(F32)
        if d:
            y_s[d - 1] = part.astype(BF16)
            along = pltpu.make_async_remote_copy(
                src_ref=y_s.at[d - 1], dst_ref=y_r.at[d - 1], send_sem=y_ss.at[d - 1], recv_sem=y_rs.at[d - 1],
                device_id=(page, yq * 2 + cc), device_id_type=MESH)
            along.start()
            sends.append(along)
        else:
            total = part
    for d in range(1, ny):
        pltpu.make_async_remote_copy(
            src_ref=y_s.at[d - 1], dst_ref=y_r.at[d - 1], send_sem=y_ss.at[d - 1], recv_sem=y_rs.at[d - 1],
            device_id=(page, mate), device_id_type=MESH).wait_recv()
        total = total + y_r[d - 1].astype(F32)
    psend[...] = total.reshape(n_page, BEAMS, width).astype(BF16)
    precv[page] = psend[page]
    p_start, p_wait, p_done = page_copy(lambda p: psend.at[p], lambda p: precv.at[p], p_ss, p_rs)
    p_start()
    p_wait()
    ff = jnp.sum(precv[...].astype(F32), axis=0)
    for g in range(n_feat):
        fsend[g] = ff[g * home:(g + 1) * home]
    frecv[feat] = fsend[feat]
    f_start, f_wait, f_done = feat_copy(
        lambda p: fsend.at[p], lambda p: frecv.at[p], lambda p: f_ss.at[p], lambda p: f_rs.at[p])
    f_start()
    f_wait()
    square = jnp.zeros((home, 1), F32)
    for c in range(n_feat):
        v = frecv[c]
        square += jnp.sum(v * v, axis=1, keepdims=True)
    scale = lax.rsqrt(square / depth + EPS)
    for c in range(n_feat):
        base = jnp.zeros((home, width), F32)
        r8 = res[c]
        for g in range(n_feat):
            base = jnp.where(feat == g, r8[g * home:(g + 1) * home], base)
        v = base + frecv[c] * scale * gains_ref[2, c]
        out_ref[:, c * width:c * width + cut(c)] = v[:, 0:cut(c)].astype(BF16)

    q_done()
    st_done()
    n_done()
    lax.fori_loop(0, n_feat, lambda c, z: (pj(c)[2](), z)[1], 0)
    ag_done()
    for copy in sends:
        copy.wait_send()
    p_done()
    f_done()


def per_device(
    n_page, n_feat,
    queries, fresh_keys, fresh_values, paged_keys, paged_values, block_tables, parents, prompt_lengths,
    stream, output_matrix, attention_gain, feedforward_gain, gate_matrix, linear_matrix, down_matrix, closing_gain,
):
    depth = stream.shape[1]
    home = stream.shape[0]
    tiles = -(-depth // 128)
    width = -(-tiles // n_feat) * 128
    padded = width * n_feat
    rows = n_page * queries.shape[0]
    slots, page_len, kvw = paged_keys.shape
    hw = queries.shape[1]
    units = gate_matrix.shape[0]
    ny = n_feat // 2
    sb = slots * BEAMS

    gains = jnp.stack([attention_gain, feedforward_gain, closing_gain]).astype(F32)
    gains = jnp.pad(gains, ((0, 0), (0, padded - depth))).reshape(3, n_feat, 1, width)

    dma = pltpu.SemaphoreType.DMA
    scratch = [
        pltpu.VMEM(paged_keys.shape, BF16), pltpu.VMEM(paged_values.shape, BF16),
        pltpu.VMEM((n_feat, width, hw), BF16),
        pltpu.VMEM((n_feat, units, width), BF16), pltpu.VMEM((n_feat, units, width), BF16),
        pltpu.VMEM((n_feat, units, width), BF16),
        pltpu.VMEM((rows, block_tables.shape[1]), jnp.int32), pltpu.VMEM((rows, HEAD), jnp.int32),
        pltpu.VMEM((n_page, BEAMS, hw), BF16),
        pltpu.VMEM((sb, hw), F32),
        pltpu.VMEM((sb, HEAD), F32),
        pltpu.VMEM((sb, hw), F32),
        pltpu.VMEM((sb, HEAD), F32),
        pltpu.VMEM((n_page, BEAMS, hw + 2 * HEAD), BF16),
        pltpu.VMEM((n_page, BEAMS, hw + 2 * HEAD), BF16),
        pltpu.VMEM((BEAMS, hw), BF16),
        pltpu.VMEM((n_feat, home, padded), F32),
        pltpu.VMEM((n_feat, n_feat, BEAMS, width), BF16),
        pltpu.VMEM((n_feat, BEAMS, width), F32),
        pltpu.VMEM((n_feat, n_page, BEAMS, width), BF16),
        pltpu.VMEM((rows, width), BF16),
        pltpu.VMEM((rows, units), F32), pltpu.VMEM((rows, units), F32),
        pltpu.VMEM((rows, units), BF16),
        pltpu.VMEM((ny, rows, width), BF16), pltpu.VMEM((ny, rows, width), BF16),
        pltpu.VMEM((ny - 1, rows, width), BF16), pltpu.VMEM((ny - 1, rows, width), BF16),
        pltpu.VMEM((n_page, BEAMS, width), BF16), pltpu.VMEM((n_page, BEAMS, width), BF16),
        pltpu.VMEM((n_feat, home, width), F32), pltpu.VMEM((n_feat, home, width), F32),
        dma((2,)), dma((4, n_feat)),
        dma((n_page,)), dma((n_page,)),
        dma((n_page,)), dma((n_page,)),
        dma((n_feat,)), dma((n_feat,)),
        dma((n_feat, n_feat)), dma((n_feat, n_feat)),
        dma((n_page,)), dma((n_page,)),
        dma((ny,)), dma((ny,)), dma((n_feat,)),
        dma((ny,)), dma((ny,)), dma((ny - 1,)), dma((ny - 1,)),
        dma((n_page,)), dma((n_page,)),
        dma((n_feat,)), dma((n_feat,)),
    ]
    vmem = pl.BlockSpec(memory_space=pltpu.VMEM)
    smem = pl.BlockSpec(memory_space=pltpu.SMEM)
    hbm = pl.BlockSpec(memory_space=pl.ANY)
    return pl.pallas_call(
        functools.partial(layer_kernel, n_page, n_feat, width, depth),
        out_shape=jax.ShapeDtypeStruct((home, depth), BF16),
        in_specs=[vmem] * 4 + [smem] * 2 + [vmem] * 2 + [hbm] * 6,
        out_specs=vmem,
        scratch_shapes=scratch,
        compiler_params=pltpu.CompilerParams(
            collective_id=0, has_side_effects=True, vmem_limit_bytes=60 * 2**20),
    )(queries, fresh_keys, fresh_values, block_tables, parents, prompt_lengths, stream, gains,
      paged_keys, paged_values, output_matrix, gate_matrix, linear_matrix, down_matrix)


def solution(mesh):
    both = P(("page", "feat"), None)
    placed = (
        P("page", "feat"), P("page", "feat"), P("page", "feat"),
        P("page", None, "feat"), P("page", None, "feat"),
        P(), P(), P(), both, P(None, "feat"), P(), P(), both, both, both, P(),
    )
    return jax.shard_map(
        functools.partial(per_device, mesh.shape["page"], mesh.shape["feat"]),
        mesh=mesh, in_specs=placed, out_specs=both, check_vma=False)
```

```python
import functools
import math

import jax
import jax.numpy as jnp
from jax import lax
from jax.experimental import pallas as pl
from jax.experimental.pallas import tpu as pltpu
from jax.sharding import PartitionSpec as P

HEAD = 128
QSCALAR = 144
SOFTCAP = 50
BEAMS = 8
EPS = 1e-06

F32 = jnp.float32
BF16 = jnp.bfloat16
MESH = pl.DeviceIdType.MESH
NT = (((1,), (1,)), ((), ()))
NN = (((1,), (0,)), ((), ()))
TN = (((0,), (0,)), ((), ()))


def capped_exp(raw):
    return jnp.exp(SOFTCAP * jnp.tanh(raw * (1.0 / (math.sqrt(QSCALAR) * SOFTCAP))))


def mm(a, b, dims):
    return lax.dot_general(a, b, dims, preferred_element_type=F32)


def layer_kernel(
    n_page, n_feat, width, depth,
    q_ref, fk_ref, fv_ref, tables_ref, parents_ref, lengths_ref, stream_ref, gains_ref,
    keys_hbm, values_hbm, wo_hbm, gate_hbm, lift_hbm, down_hbm,
    out_ref,
    kbuf, vbuf, wo, gate, lift, down,
    allq, qs, nvs, snum, stot, nsend, nrecv, att, strm, prj, res,
    xg, xs, gacc, uacc, hid, core_s, core_r, y_s, y_r, psend, precv, fsend, frecv,
    kv_sem, w_sem,
    q_ss, q_rs, n_ss, n_rs, st_ss, st_rs, pj_ss, pj_rs, ag_ss, ag_rs,
    xy_ss, xc_ss, x_rs, c_ss, c_rs, y_ss, y_rs, p_ss, p_rs, f_ss, f_rs,
):
    page = lax.axis_index("page")
    feat = lax.axis_index("feat")
    ny = n_feat // 2
    yy, cc = feat // 2, feat % 2
    mate = yy * 2 + (1 - cc)
    slots, page_len, kvw = kbuf.shape
    kv_heads = kvw // HEAD
    heads = q_ref.shape[1] // HEAD
    groups = heads // kv_heads
    rows = n_page * BEAMS
    home = stream_ref.shape[0]
    hw = heads * HEAD

    def gain(i, c):
        first = (i * n_feat + c) * width
        return gains_ref[:, first:first + width]

    def cut(c):
        return min(width, depth - c * width)

    local = [
        pltpu.make_async_copy(keys_hbm, kbuf, kv_sem.at[0]),
        pltpu.make_async_copy(values_hbm, vbuf, kv_sem.at[1]),
    ]
    w_copies = [[], [], [], []]
    for c in range(n_feat):
        part = pl.ds(c * width, cut(c))
        have = pl.ds(0, cut(c))
        w_copies[0].append(pltpu.make_async_copy(wo_hbm.at[part, :], wo.at[c, have, :], w_sem.at[0, c]))
        w_copies[1].append(pltpu.make_async_copy(gate_hbm.at[:, part], gate.at[c, :, have], w_sem.at[1, c]))
        w_copies[2].append(pltpu.make_async_copy(lift_hbm.at[:, part], lift.at[c, :, have], w_sem.at[2, c]))
        w_copies[3].append(pltpu.make_async_copy(down_hbm.at[:, part], down.at[c, :, have], w_sem.at[3, c]))
        if cut(c) < width:
            rest = width - cut(c)
            wo[c, cut(c):, :] = jnp.zeros((rest, wo.shape[2]), BF16)
            gate[c, :, cut(c):] = jnp.zeros((gate.shape[1], rest), BF16)
            lift[c, :, cut(c):] = jnp.zeros((gate.shape[1], rest), BF16)
            down[c, :, cut(c):] = jnp.zeros((gate.shape[1], rest), BF16)
    for copy in local:
        copy.start()

    barrier = pltpu.get_barrier_semaphore()

    def greet_page(d, _):
        pl.semaphore_signal(barrier, inc=1, device_id=((page + d) % n_page, feat), device_id_type=MESH)
        return 0

    def greet_feat(d, _):
        pl.semaphore_signal(barrier, inc=1, device_id=(page, (feat + d) % n_feat), device_id_type=MESH)
        return 0

    lax.fori_loop(1, n_page, greet_page, 0)
    lax.fori_loop(1, n_feat, greet_feat, 0)

    allq[page] = q_ref[...]
    sf = stream_ref[...].astype(F32)
    if strm.shape[2] > depth:
        sf = jnp.concatenate([sf, jnp.zeros((home, strm.shape[2] - depth), F32)], axis=1)
    strm[feat] = sf
    pl.semaphore_wait(barrier, n_page + n_feat - 2)

    def page_copy(src, dst, ss, rs):
        def send(d):
            peer = (page + d) % n_page
            return pltpu.make_async_remote_copy(
                src_ref=src(peer), dst_ref=dst(page), send_sem=ss.at[peer], recv_sem=rs.at[page],
                device_id=(peer, feat), device_id_type=MESH)

        def arrival(d):
            peer = (page + d) % n_page
            return pltpu.make_async_remote_copy(
                src_ref=src(peer), dst_ref=dst(peer), send_sem=ss.at[peer], recv_sem=rs.at[peer],
                device_id=(peer, feat), device_id_type=MESH)

        def start():
            lax.fori_loop(1, n_page, lambda d, z: (send(d).start(), z)[1], 0)

        def wait_recv():
            lax.fori_loop(1, n_page, lambda d, z: (arrival(d).wait_recv(), z)[1], 0)

        def wait_send():
            lax.fori_loop(1, n_page, lambda d, z: (send(d).wait_send(), z)[1], 0)

        return start, wait_recv, wait_send

    def feat_copy(src, dst, ss, rs):
        def send(d):
            peer = (feat + d) % n_feat
            return pltpu.make_async_remote_copy(
                src_ref=src(peer), dst_ref=dst(feat), send_sem=ss(peer), recv_sem=rs(feat),
                device_id=(page, peer), device_id_type=MESH)

        def arrival(d):
            peer = (feat + d) % n_feat
            return pltpu.make_async_remote_copy(
                src_ref=src(peer), dst_ref=dst(peer), send_sem=ss(peer), recv_sem=rs(peer),
                device_id=(page, peer), device_id_type=MESH)

        def start():
            lax.fori_loop(1, n_feat, lambda d, z: (send(d).start(), z)[1], 0)

        def wait_recv():
            lax.fori_loop(1, n_feat, lambda d, z: (arrival(d).wait_recv(), z)[1], 0)

        def wait_send():
            lax.fori_loop(1, n_feat, lambda d, z: (send(d).wait_send(), z)[1], 0)

        return start, wait_recv, wait_send

    q_start, q_wait, q_done = page_copy(lambda p: allq.at[page], lambda p: allq.at[p], q_ss, q_rs)
    q_start()
    st_start, st_wait, st_done = feat_copy(
        lambda p: strm.at[feat], lambda p: strm.at[p], lambda p: st_ss.at[p], lambda p: st_rs.at[p])
    st_start()

    blocks = tables_ref.shape[0]
    prompts = lengths_ref.shape[1]
    sb = slots * BEAMS
    chosen = lax.broadcasted_iota(jnp.int32, (rows, rows), 0) == parents_ref[...]
    by_col = lax.dot_general(tables_ref[...].astype(F32), jnp.where(chosen, 1.0, 0.0), NN,
                             precision=lax.Precision.HIGHEST, preferred_element_type=F32)
    of_prompt = (lax.broadcasted_iota(jnp.int32, (prompts, rows), 0)
                 == lax.broadcasted_iota(jnp.int32, (prompts, rows), 1) // BEAMS)
    lens = lax.dot_general(lengths_ref[...].astype(F32), jnp.where(of_prompt, 1.0, 0.0), NN,
                           precision=lax.Precision.HIGHEST, preferred_element_type=F32)
    spot_i = lax.broadcasted_iota(jnp.int32, (sb, rows), 0)
    row_i = lax.broadcasted_iota(jnp.int32, (sb, rows), 1)
    slot_id = (page * slots + spot_i // BEAMS).astype(F32)
    seen = jnp.zeros((sb, rows), F32)
    for b in range(blocks):
        seen += jnp.where(jnp.abs(by_col[b:b + 1, :] - slot_id) < 0.5,
                          jnp.clip(lens - b * page_len, 0.0, float(page_len)), 0.0)
    seen = jnp.where(spot_i % BEAMS == row_i % BEAMS, seen, 0.0)
    pick = jnp.where(seen > 0, 1.0, 0.0).astype(BF16)
    nvs[...] = jnp.broadcast_to(jnp.sum(seen, axis=1, keepdims=True), nvs.shape)

    q_wait()
    q_all = allq[...].astype(F32).reshape(rows, hw).astype(BF16)
    qs[...] = mm(pick, q_all, NN)
    for copy in local:
        copy.wait()
    for kind in w_copies:
        for copy in kind:
            copy.start()

    lane = lax.broadcasted_iota(jnp.int32, (BEAMS, HEAD), 1)
    position = lax.broadcasted_iota(jnp.int32, (groups * BEAMS, page_len), 1).astype(F32)

    def one_slot(s):
        at = pl.ds(pl.multiple_of(s * BEAMS, BEAMS), BEAMS)
        limit = jnp.concatenate([nvs[at, :]] * groups, axis=0)[:, 0:1]
        visible = position < limit
        sums = jnp.zeros((BEAMS, HEAD), F32)
        for k in range(kv_heads):
            kv = slice(k * HEAD, (k + 1) * HEAD)
            qk = jnp.concatenate(
                [qs[at, (k * groups + g) * HEAD:(k * groups + g + 1) * HEAD] for g in range(groups)], axis=0)
            raw = mm(qk.astype(BF16), kbuf[s, :, kv], NT)
            w = jnp.where(visible, capped_exp(raw), 0.0)
            tot = jnp.sum(w, axis=1, keepdims=True)
            num = mm(w.astype(BF16), vbuf[s, :, kv], NN)
            for g in range(groups):
                h = k * groups + g
                snum[at, h * HEAD:(h + 1) * HEAD] = num[g * BEAMS:(g + 1) * BEAMS]
                sums = jnp.where(lane == h, tot[g * BEAMS:(g + 1) * BEAMS], sums)
        stot[at, :] = sums

    per = 2 if slots % 2 == 0 else 1

    def some_slots(i, z):
        for u in range(per):
            one_slot(i * per + u)
        return z

    lax.fori_loop(0, slots // per, some_slots, 0)

    def to_rows(v):
        hi = v.astype(BF16)
        lo = (v - hi.astype(F32)).astype(BF16)
        return mm(pick, hi, TN) + mm(pick, lo, TN)

    tot_rows = to_rows(stot[...])
    tot_hi = tot_rows.astype(BF16)
    tot_lo = tot_rows - tot_hi.astype(F32)
    nsend[:, :, 0:hw] = to_rows(snum[...]).reshape(n_page, BEAMS, hw).astype(BF16)
    nsend[:, :, hw:hw + HEAD] = tot_hi.astype(F32).reshape(n_page, BEAMS, HEAD).astype(BF16)
    nsend[:, :, hw + HEAD:hw + 2 * HEAD] = tot_lo.reshape(n_page, BEAMS, HEAD).astype(BF16)
    nrecv[page] = nsend[page]
    n_start, n_wait, n_done = page_copy(lambda p: nsend.at[p], lambda p: nrecv.at[p], n_ss, n_rs)
    n_start()

    own_w = []
    for h in range(heads):
        k = h // groups
        qk = q_ref[:, h * HEAD:(h + 1) * HEAD].astype(F32) * fk_ref[:, k * HEAD:(k + 1) * HEAD].astype(F32)
        own_w.append(capped_exp(jnp.sum(qk, axis=1, keepdims=True)))
    n_wait()
    totals = jnp.sum(nrecv[:, :, hw:hw + HEAD].astype(F32) + nrecv[:, :, hw + HEAD:hw + 2 * HEAD].astype(F32), axis=0)
    for h in range(heads):
        k = h // groups
        hs = slice(h * HEAD, (h + 1) * HEAD)
        num = jnp.sum(nrecv[:, :, hs].astype(F32), axis=0)
        num += own_w[h].astype(BF16).astype(F32) * fv_ref[:, k * HEAD:(k + 1) * HEAD].astype(F32)
        att[:, hs] = (num / (totals[:, h:h + 1] + own_w[h])).astype(BF16)

    for copy in w_copies[0]:
        copy.wait()

    def pj(c):
        return feat_copy(lambda p: prj.at[feat, c], lambda p: prj.at[p, c],
                         lambda p: pj_ss.at[p, c], lambda p: pj_rs.at[p, c])

    def project(c, z):
        prj[feat, c] = mm(att[...], wo[c], NT).astype(BF16)
        pj(c)[0]()
        return z

    lax.fori_loop(0, n_feat, project, 0)
    st_wait()
    lax.fori_loop(0, n_feat, lambda c, z: (pj(c)[1](), z)[1], 0)

    square = jnp.zeros((BEAMS, 1), F32)
    for c in range(n_feat):
        v = jnp.sum(prj[:, c].astype(F32), axis=0)
        res[c] = v
        square += jnp.sum(v * v, axis=1, keepdims=True)
    scale = lax.rsqrt(square / depth + EPS)
    square = jnp.zeros((BEAMS, 1), F32)
    for c in range(n_feat):
        cols = slice(c * width, (c + 1) * width)
        base = jnp.concatenate([strm[g, :, cols] for g in range(n_feat)], axis=0)
        v = base + res[c] * scale * gain(0, c)
        res[c] = v
        square += jnp.sum(v * v, axis=1, keepdims=True)
    scale = lax.rsqrt(square / depth + EPS)
    own_gain = gain(1, 0)
    for c in range(1, n_feat):
        own_gain = jnp.where(feat == c, gain(1, c), own_gain)
    xg[feat, page] = (res[feat] * scale * own_gain).astype(BF16)

    ag_start, ag_wait, ag_done = page_copy(
        lambda p: xg.at[feat, page], lambda p: xg.at[feat, p], ag_ss, ag_rs)
    ag_start()
    for kind in w_copies[1:3]:
        for copy in kind:
            copy.wait()

    def chunk_copy(q, peer, ss):
        return pltpu.make_async_remote_copy(
            src_ref=xg.at[q], dst_ref=xg.at[q], send_sem=ss, recv_sem=x_rs.at[q],
            device_id=(page, peer), device_id_type=MESH)

    ag_wait()
    sends = []
    for d in range(1, ny):
        sends.append(chunk_copy(feat, ((yy + d) % ny) * 2 + cc, xy_ss.at[d]))
        sends[-1].start()
    sends.append(chunk_copy(feat, mate, xc_ss.at[0]))
    sends[-1].start()
    for d in range(ny):
        for o in range(2):
            q = ((yy + ny - d) % ny) * 2 + (cc if o == 0 else 1 - cc)
            if d or o:
                chunk_copy(q, mate, xc_ss.at[d]).wait_recv()
            if d and not o:
                sends.append(chunk_copy(q, mate, xc_ss.at[d]))
                sends[-1].start()
            xs[...] = xg[q].astype(F32).reshape(rows, width).astype(BF16)
            if d or o:
                gacc[...] += mm(gate[q], xs[...], NT)
                uacc[...] += mm(lift[q], xs[...], NT)
            else:
                gacc[...] = mm(gate[q], xs[...], NT)
                uacc[...] = mm(lift[q], xs[...], NT)
    turned = (jax.nn.gelu(gacc[...], approximate=True) * uacc[...]).astype(BF16)
    eye = jnp.where(lax.broadcasted_iota(jnp.int32, (rows, rows), 0)
                    == lax.broadcasted_iota(jnp.int32, (rows, rows), 1), 1.0, 0.0).astype(BF16)
    hid[...] = mm(eye, turned, NT).astype(BF16)

    for copy in w_copies[3]:
        copy.wait()
    total = None
    for d in list(range(1, ny)) + [0]:
        yq = (yy + d) % ny
        core_s[d] = mm(hid[...], down[yq * 2 + (1 - cc)], NN).astype(BF16)
        over = pltpu.make_async_remote_copy(
            src_ref=core_s.at[d], dst_ref=core_r.at[d], send_sem=c_ss.at[d], recv_sem=c_rs.at[d],
            device_id=(page, mate), device_id_type=MESH)
        over.start()
        sends.append(over)
        part = mm(hid[...], down[yq * 2 + cc], NN)
        over.wait_recv()
        part = part + core_r[d].astype(F32)
        if d:
            y_s[d - 1] = part.astype(BF16)
            along = pltpu.make_async_remote_copy(
                src_ref=y_s.at[d - 1], dst_ref=y_r.at[d - 1], send_sem=y_ss.at[d - 1], recv_sem=y_rs.at[d - 1],
                device_id=(page, yq * 2 + cc), device_id_type=MESH)
            along.start()
            sends.append(along)
        else:
            total = part
    for d in range(1, ny):
        pltpu.make_async_remote_copy(
            src_ref=y_s.at[d - 1], dst_ref=y_r.at[d - 1], send_sem=y_ss.at[d - 1], recv_sem=y_rs.at[d - 1],
            device_id=(page, mate), device_id_type=MESH).wait_recv()
        total = total + y_r[d - 1].astype(F32)
    psend[...] = total.reshape(n_page, BEAMS, width).astype(BF16)
    precv[page] = psend[page]
    p_start, p_wait, p_done = page_copy(lambda p: psend.at[p], lambda p: precv.at[p], p_ss, p_rs)
    p_start()
    p_wait()
    ff = jnp.sum(precv[...].astype(F32), axis=0)
    for g in range(n_feat):
        fsend[g] = ff[g * home:(g + 1) * home]
    frecv[feat] = fsend[feat]
    f_start, f_wait, f_done = feat_copy(
        lambda p: fsend.at[p], lambda p: frecv.at[p], lambda p: f_ss.at[p], lambda p: f_rs.at[p])
    f_start()
    f_wait()
    square = jnp.zeros((home, 1), F32)
    for c in range(n_feat):
        v = frecv[c]
        square += jnp.sum(v * v, axis=1, keepdims=True)
    scale = lax.rsqrt(square / depth + EPS)
    for c in range(n_feat):
        base = jnp.zeros((home, width), F32)
        r8 = res[c]
        for g in range(n_feat):
            base = jnp.where(feat == g, r8[g * home:(g + 1) * home], base)
        v = base + frecv[c] * scale * gain(2, c)
        out_ref[:, c * width:c * width + cut(c)] = v[:, 0:cut(c)].astype(BF16)

    q_done()
    st_done()
    n_done()
    lax.fori_loop(0, n_feat, lambda c, z: (pj(c)[2](), z)[1], 0)
    ag_done()
    for copy in sends:
        copy.wait_send()
    p_done()
    f_done()


def per_device(
    n_page, n_feat,
    queries, fresh_keys, fresh_values, paged_keys, paged_values, block_tables, parents, prompt_lengths,
    stream, output_matrix, attention_gain, feedforward_gain, gate_matrix, linear_matrix, down_matrix, closing_gain,
):
    depth = stream.shape[1]
    home = stream.shape[0]
    tiles = -(-depth // 128)
    width = -(-tiles // n_feat) * 128
    padded = width * n_feat
    rows = n_page * queries.shape[0]
    slots, page_len, kvw = paged_keys.shape
    hw = queries.shape[1]
    units = gate_matrix.shape[0]
    ny = n_feat // 2
    sb = slots * BEAMS

    gains = jnp.concatenate([
        jnp.pad(g.astype(F32), (0, padded - depth)) if padded > depth else g.astype(F32)
        for g in (attention_gain, feedforward_gain, closing_gain)]).reshape(1, -1)

    dma = pltpu.SemaphoreType.DMA
    scratch = [
        pltpu.VMEM(paged_keys.shape, BF16), pltpu.VMEM(paged_values.shape, BF16),
        pltpu.VMEM((n_feat, width, hw), BF16),
        pltpu.VMEM((n_feat, units, width), BF16), pltpu.VMEM((n_feat, units, width), BF16),
        pltpu.VMEM((n_feat, units, width), BF16),
        pltpu.VMEM((n_page, BEAMS, hw), BF16),
        pltpu.VMEM((sb, hw), F32),
        pltpu.VMEM((sb, HEAD), F32),
        pltpu.VMEM((sb, hw), F32),
        pltpu.VMEM((sb, HEAD), F32),
        pltpu.VMEM((n_page, BEAMS, hw + 2 * HEAD), BF16),
        pltpu.VMEM((n_page, BEAMS, hw + 2 * HEAD), BF16),
        pltpu.VMEM((BEAMS, hw), BF16),
        pltpu.VMEM((n_feat, home, padded), F32),
        pltpu.VMEM((n_feat, n_feat, BEAMS, width), BF16),
        pltpu.VMEM((n_feat, BEAMS, width), F32),
        pltpu.VMEM((n_feat, n_page, BEAMS, width), BF16),
        pltpu.VMEM((rows, width), BF16),
        pltpu.VMEM((units, rows), F32), pltpu.VMEM((units, rows), F32),
        pltpu.VMEM((rows, units), BF16),
        pltpu.VMEM((ny, rows, width), BF16), pltpu.VMEM((ny, rows, width), BF16),
        pltpu.VMEM((ny - 1, rows, width), BF16), pltpu.VMEM((ny - 1, rows, width), BF16),
        pltpu.VMEM((n_page, BEAMS, width), BF16), pltpu.VMEM((n_page, BEAMS, width), BF16),
        pltpu.VMEM((n_feat, home, width), F32), pltpu.VMEM((n_feat, home, width), F32),
        dma((2,)), dma((4, n_feat)),
        dma((n_page,)), dma((n_page,)),
        dma((n_page,)), dma((n_page,)),
        dma((n_feat,)), dma((n_feat,)),
        dma((n_feat, n_feat)), dma((n_feat, n_feat)),
        dma((n_page,)), dma((n_page,)),
        dma((ny,)), dma((ny,)), dma((n_feat,)),
        dma((ny,)), dma((ny,)), dma((ny - 1,)), dma((ny - 1,)),
        dma((n_page,)), dma((n_page,)),
        dma((n_feat,)), dma((n_feat,)),
    ]
    vmem = pl.BlockSpec(memory_space=pltpu.VMEM)
    hbm = pl.BlockSpec(memory_space=pl.ANY)
    return pl.pallas_call(
        functools.partial(layer_kernel, n_page, n_feat, width, depth),
        out_shape=jax.ShapeDtypeStruct((home, depth), BF16),
        in_specs=[vmem] * 8 + [hbm] * 6,
        out_specs=vmem,
        scratch_shapes=scratch,
        compiler_params=pltpu.CompilerParams(
            collective_id=0, has_side_effects=True, vmem_limit_bytes=60 * 2**20),
    )(queries, fresh_keys, fresh_values, block_tables.T, parents.reshape(1, -1),
      prompt_lengths.reshape(1, -1), stream, gains,
      paged_keys, paged_values, output_matrix, gate_matrix, linear_matrix, down_matrix)


def solution(mesh):
    both = P(("page", "feat"), None)
    placed = (
        P("page", "feat"), P("page", "feat"), P("page", "feat"),
        P("page", None, "feat"), P("page", None, "feat"),
        P(), P(), P(), both, P(None, "feat"), P(), P(), both, both, both, P(),
    )
    return jax.shard_map(
        functools.partial(per_device, mesh.shape["page"], mesh.shape["feat"]),
        mesh=mesh, in_specs=placed, out_specs=both, check_vma=False)
```

```python
import functools
import math

import jax
import jax.numpy as jnp
from jax import lax
from jax.experimental import pallas as pl
from jax.experimental.pallas import tpu as pltpu
from jax.sharding import PartitionSpec as P

HEAD = 128
QSCALAR = 144
SOFTCAP = 50
BEAMS = 8
EPS = 1e-06

F32 = jnp.float32
BF16 = jnp.bfloat16
MESH = pl.DeviceIdType.MESH
NT = (((1,), (1,)), ((), ()))
NN = (((1,), (0,)), ((), ()))
TN = (((0,), (0,)), ((), ()))


def capped_exp(raw):
    return jnp.exp(SOFTCAP * jnp.tanh(raw * (1.0 / (math.sqrt(QSCALAR) * SOFTCAP))))


def ahead(i, d, n):
    return jnp.where(i + d >= n, i + d - n, i + d)


def halves(width):
    first = width // 512 * 256
    return ((0, first), (first, width - first)) if first else ((0, width),)


def mm(a, b, dims):
    return lax.dot_general(a, b, dims, preferred_element_type=F32)


def layer_kernel(
    n_page, n_feat, width, depth,
    q_ref, fk_ref, fv_ref, tables_ref, parents_ref, lengths_ref, stream_ref, gains_ref,
    keys_hbm, values_hbm, wo_hbm, gate_hbm, lift_hbm, down_hbm,
    out_ref,
    kbuf, vbuf, wo, gate, lift, down,
    allq, qs, nvs, snum, stot, nsend, nrecv, att, strm, prj, res,
    xg, gacc, uacc, hid, core_s, core_r, y_s, y_r, psend, precv, fsend, frecv,
    kv_sem, w_sem,
    q_ss, q_rs, n_ss, n_rs, st_ss, st_rs, pj_ss, pj_rs, ag_ss, ag_rs,
    xy_ss, xc_ss, x_rs, c_ss, c_rs, y_ss, y_rs, p_ss, p_rs, f_ss, f_rs,
):
    page = lax.axis_index("page")
    feat = lax.axis_index("feat")
    ny = n_feat // 2
    yy, cc = feat // 2, feat % 2
    mate = yy * 2 + (1 - cc)
    slots, page_len, kvw = kbuf.shape
    kv_heads = kvw // HEAD
    heads = q_ref.shape[1] // HEAD
    groups = heads // kv_heads
    rows = n_page * BEAMS
    home = stream_ref.shape[0]
    hw = heads * HEAD

    spans = [pl.ds(first, size) for first, size in halves(width)]
    parts = len(spans)

    def gain(i, c):
        first = (i * n_feat + c) * width
        return gains_ref[:, first:first + width]

    def cut(c):
        return min(width, depth - c * width)

    local = [
        pltpu.make_async_copy(keys_hbm, kbuf, kv_sem.at[0]),
        pltpu.make_async_copy(values_hbm, vbuf, kv_sem.at[1]),
    ]
    w_copies = [[], [], [], []]
    for c in range(n_feat):
        part = pl.ds(c * width, cut(c))
        have = pl.ds(0, cut(c))
        w_copies[0].append(pltpu.make_async_copy(wo_hbm.at[part, :], wo.at[c, have, :], w_sem.at[0, c]))
        w_copies[1].append(pltpu.make_async_copy(gate_hbm.at[:, part], gate.at[c, :, have], w_sem.at[1, c]))
        w_copies[2].append(pltpu.make_async_copy(lift_hbm.at[:, part], lift.at[c, :, have], w_sem.at[2, c]))
        w_copies[3].append(pltpu.make_async_copy(down_hbm.at[:, part], down.at[c, :, have], w_sem.at[3, c]))
        if cut(c) < width:
            rest = width - cut(c)
            wo[c, cut(c):, :] = jnp.zeros((rest, wo.shape[2]), BF16)
            gate[c, :, cut(c):] = jnp.zeros((gate.shape[1], rest), BF16)
            lift[c, :, cut(c):] = jnp.zeros((gate.shape[1], rest), BF16)
            down[c, :, cut(c):] = jnp.zeros((gate.shape[1], rest), BF16)
    for copy in local:
        copy.start()

    barrier = pltpu.get_barrier_semaphore()

    def greet_page(d, _):
        pl.semaphore_signal(barrier, inc=1, device_id=(ahead(page, d, n_page), feat), device_id_type=MESH)
        return 0

    def greet_feat(d, _):
        pl.semaphore_signal(barrier, inc=1, device_id=(page, ahead(feat, d, n_feat)), device_id_type=MESH)
        return 0

    lax.fori_loop(1, n_page, greet_page, 0)
    lax.fori_loop(1, n_feat, greet_feat, 0)

    allq[page] = q_ref[...]
    sf = stream_ref[...].astype(F32)
    if strm.shape[2] > depth:
        sf = jnp.concatenate([sf, jnp.zeros((home, strm.shape[2] - depth), F32)], axis=1)
    strm[feat] = sf
    pl.semaphore_wait(barrier, n_page + n_feat - 2)

    def page_copy(src, dst, ss, rs):
        def send(d):
            peer = ahead(page, d, n_page)
            return pltpu.make_async_remote_copy(
                src_ref=src(peer), dst_ref=dst(page), send_sem=ss.at[peer], recv_sem=rs.at[page],
                device_id=(peer, feat), device_id_type=MESH)

        def arrival(d):
            peer = ahead(page, d, n_page)
            return pltpu.make_async_remote_copy(
                src_ref=src(peer), dst_ref=dst(peer), send_sem=ss.at[peer], recv_sem=rs.at[peer],
                device_id=(peer, feat), device_id_type=MESH)

        def start():
            lax.fori_loop(1, n_page, lambda d, z: (send(d).start(), z)[1], 0, unroll=n_page <= 8)

        def wait_recv():
            lax.fori_loop(1, n_page, lambda d, z: (arrival(d).wait_recv(), z)[1], 0, unroll=n_page <= 8)

        def wait_send():
            lax.fori_loop(1, n_page, lambda d, z: (send(d).wait_send(), z)[1], 0, unroll=n_page <= 8)

        return start, wait_recv, wait_send

    def feat_copy(src, dst, ss, rs):
        def send(d):
            peer = ahead(feat, d, n_feat)
            return pltpu.make_async_remote_copy(
                src_ref=src(peer), dst_ref=dst(feat), send_sem=ss(peer), recv_sem=rs(feat),
                device_id=(page, peer), device_id_type=MESH)

        def arrival(d):
            peer = ahead(feat, d, n_feat)
            return pltpu.make_async_remote_copy(
                src_ref=src(peer), dst_ref=dst(peer), send_sem=ss(peer), recv_sem=rs(peer),
                device_id=(page, peer), device_id_type=MESH)

        def start():
            lax.fori_loop(1, n_feat, lambda d, z: (send(d).start(), z)[1], 0, unroll=n_feat <= 8)

        def wait_recv():
            lax.fori_loop(1, n_feat, lambda d, z: (arrival(d).wait_recv(), z)[1], 0, unroll=n_feat <= 8)

        def wait_send():
            lax.fori_loop(1, n_feat, lambda d, z: (send(d).wait_send(), z)[1], 0, unroll=n_feat <= 8)

        return start, wait_recv, wait_send

    q_start, q_wait, q_done = page_copy(lambda p: allq.at[page], lambda p: allq.at[p], q_ss, q_rs)
    q_start()
    st_start, st_wait, st_done = feat_copy(
        lambda p: strm.at[feat], lambda p: strm.at[p], lambda p: st_ss.at[p], lambda p: st_rs.at[p])
    st_start()

    blocks = tables_ref.shape[0]
    prompts = lengths_ref.shape[1]
    sb = slots * BEAMS
    chosen = lax.broadcasted_iota(jnp.int32, (rows, rows), 0) == parents_ref[...]
    by_col = lax.dot_general(tables_ref[...].astype(F32), jnp.where(chosen, 1.0, 0.0), NN,
                             precision=lax.Precision.HIGHEST, preferred_element_type=F32)
    of_prompt = (lax.broadcasted_iota(jnp.int32, (prompts, rows), 0)
                 == lax.broadcasted_iota(jnp.int32, (prompts, rows), 1) // BEAMS)
    lens = lax.dot_general(lengths_ref[...].astype(F32), jnp.where(of_prompt, 1.0, 0.0), NN,
                           precision=lax.Precision.HIGHEST, preferred_element_type=F32)
    spot_i = lax.broadcasted_iota(jnp.int32, (sb, rows), 0)
    row_i = lax.broadcasted_iota(jnp.int32, (sb, rows), 1)
    slot_id = (page * slots + spot_i // BEAMS).astype(F32)
    seen = jnp.zeros((sb, rows), F32)
    for b in range(blocks):
        seen += jnp.where(jnp.abs(by_col[b:b + 1, :] - slot_id) < 0.5,
                          jnp.clip(lens - b * page_len, 0.0, float(page_len)), 0.0)
    seen = jnp.where(spot_i % BEAMS == row_i % BEAMS, seen, 0.0)
    pick = jnp.where(seen > 0, 1.0, 0.0).astype(BF16)
    nvs[...] = jnp.broadcast_to(jnp.sum(seen, axis=1, keepdims=True), nvs.shape)

    q_wait()
    q_all = allq[...].astype(F32).reshape(rows, hw).astype(BF16)
    qs[...] = mm(pick, q_all, NN)
    for copy in local:
        copy.wait()
    for kind in w_copies:
        for copy in kind:
            copy.start()

    half_lanes = HEAD // 2
    lane = lax.broadcasted_iota(jnp.int32, (BEAMS, HEAD), 1)
    position = lax.broadcasted_iota(jnp.int32, (groups * BEAMS, page_len), 1).astype(F32)

    def one_slot(s):
        at = pl.ds(pl.multiple_of(s * BEAMS, BEAMS), BEAMS)
        limit = jnp.concatenate([nvs[at, :]] * groups, axis=0)[:, 0:1]
        visible = position < limit
        sums = jnp.zeros((BEAMS, HEAD), F32)
        for k in range(kv_heads):
            kv = slice(k * HEAD, (k + 1) * HEAD)
            qk = jnp.concatenate(
                [qs[at, (k * groups + g) * HEAD:(k * groups + g + 1) * HEAD] for g in range(groups)], axis=0)
            raw = mm(qk.astype(BF16), kbuf[s, :, kv], NT)
            w = jnp.where(visible, capped_exp(raw), 0.0)
            tot = jnp.sum(w, axis=1, keepdims=True)
            num = mm(w.astype(BF16), vbuf[s, :, kv], NN)
            for g in range(groups):
                h = k * groups + g
                snum[at, h * HEAD:(h + 1) * HEAD] = num[g * BEAMS:(g + 1) * BEAMS]
                sums = jnp.where(lane % half_lanes == h, tot[g * BEAMS:(g + 1) * BEAMS], sums)
        stot[at, :] = sums

    per = 4 if slots % 4 == 0 else 1

    def some_slots(i, z):
        for u in range(per):
            one_slot(i * per + u)
        return z

    lax.fori_loop(0, slots // per, some_slots, 0)

    def to_rows(v):
        hi = v.astype(BF16)
        lo = (v - hi.astype(F32)).astype(BF16)
        return mm(pick, hi, TN) + mm(pick, lo, TN)

    tot_rows = to_rows(stot[...])
    tot_hi = tot_rows.astype(BF16).astype(F32)
    first = lax.broadcasted_iota(jnp.int32, tot_rows.shape, 1) < half_lanes
    tot_both = jnp.where(first, tot_hi, tot_rows - tot_hi)
    nsend[:, :, 0:hw] = to_rows(snum[...]).reshape(n_page, BEAMS, hw).astype(BF16)
    nsend[:, :, hw:hw + HEAD] = tot_both.reshape(n_page, BEAMS, HEAD).astype(BF16)
    nrecv[page] = nsend[page]
    n_start, n_wait, n_done = page_copy(lambda p: nsend.at[p], lambda p: nrecv.at[p], n_ss, n_rs)
    n_start()

    own_w = []
    for h in range(heads):
        k = h // groups
        qk = q_ref[:, h * HEAD:(h + 1) * HEAD].astype(F32) * fk_ref[:, k * HEAD:(k + 1) * HEAD].astype(F32)
        own_w.append(capped_exp(jnp.sum(qk, axis=1, keepdims=True)))
    n_wait()
    totals = jnp.sum(nrecv[:, :, hw:hw + HEAD].astype(F32), axis=0)
    for h in range(heads):
        k = h // groups
        hs = slice(h * HEAD, (h + 1) * HEAD)
        num = jnp.sum(nrecv[:, :, hs].astype(F32), axis=0)
        num += own_w[h].astype(BF16).astype(F32) * fv_ref[:, k * HEAD:(k + 1) * HEAD].astype(F32)
        att[:, hs] = (num / (totals[:, h:h + 1] + totals[:, half_lanes + h:half_lanes + h + 1] + own_w[h])).astype(BF16)

    for copy in w_copies[0]:
        copy.wait()

    def pj(c):
        return feat_copy(lambda p: prj.at[feat, c], lambda p: prj.at[p, c],
                         lambda p: pj_ss.at[p, c], lambda p: pj_rs.at[p, c])

    def project(c, z):
        prj[feat, c] = mm(att[...], wo[c], NT).astype(BF16)
        pj(c)[0]()
        return z

    lax.fori_loop(0, n_feat, project, 0)
    st_wait()
    lax.fori_loop(0, n_feat, lambda c, z: (pj(c)[1](), z)[1], 0)

    square = jnp.zeros((BEAMS, 1), F32)
    for c in range(n_feat):
        v = jnp.sum(prj[:, c].astype(F32), axis=0)
        res[c] = v
        square += jnp.sum(v * v, axis=1, keepdims=True)
    scale = lax.rsqrt(square / depth + EPS)
    square = jnp.zeros((BEAMS, 1), F32)
    for c in range(n_feat):
        cols = slice(c * width, (c + 1) * width)
        base = jnp.concatenate([strm[g, :, cols] for g in range(n_feat)], axis=0)
        v = base + res[c] * scale * gain(0, c)
        res[c] = v
        square += jnp.sum(v * v, axis=1, keepdims=True)
    scale = lax.rsqrt(square / depth + EPS)
    own_gain = gain(1, 0)
    for c in range(1, n_feat):
        own_gain = jnp.where(feat == c, gain(1, c), own_gain)
    xg[feat, page] = (res[feat] * scale * own_gain).astype(BF16)

    def ag(i):
        return page_copy(lambda p: xg.at[feat, page, :, spans[i]], lambda p: xg.at[feat, p, :, spans[i]],
                         ag_ss.at[i], ag_rs.at[i])

    for i in range(parts):
        ag(i)[0]()
    for kind in w_copies[1:3]:
        for copy in kind:
            copy.wait()

    def chunk_copy(q, i, peer, ss):
        return pltpu.make_async_remote_copy(
            src_ref=xg.at[q, :, :, spans[i]], dst_ref=xg.at[q, :, :, spans[i]], send_sem=ss, recv_sem=x_rs.at[q, i],
            device_id=(page, peer), device_id_type=MESH)

    sends = []

    def absorb(q, i, fresh):
        sp = spans[i]
        x = xg[q, :, :, sp].astype(F32).reshape(rows, sp.size).astype(BF16)
        if fresh:
            gacc[...] = mm(x, gate[q, :, sp], NT)
            uacc[...] = mm(x, lift[q, :, sp], NT)
        else:
            gacc[...] += mm(x, gate[q, :, sp], NT)
            uacc[...] += mm(x, lift[q, :, sp], NT)

    for i in range(parts):
        ag(i)[1]()
        for d in range(1, ny):
            sends.append(chunk_copy(feat, i, ahead(yy, d, ny) * 2 + cc, xy_ss.at[d, i]))
            sends[-1].start()
        sends.append(chunk_copy(feat, i, mate, xc_ss.at[0, i]))
        sends[-1].start()
        absorb(feat, i, i == 0)
    for i in range(parts):
        chunk_copy(mate, i, mate, xc_ss.at[0, i]).wait_recv()
        absorb(mate, i, False)
    for d in range(1, ny):
        base = ahead(yy, ny - d, ny) * 2
        for i in range(parts):
            chunk_copy(base + cc, i, mate, xc_ss.at[d, i]).wait_recv()
            sends.append(chunk_copy(base + cc, i, mate, xc_ss.at[d, i]))
            sends[-1].start()
            absorb(base + cc, i, False)
        for i in range(parts):
            chunk_copy(base + 1 - cc, i, mate, xc_ss.at[d, i]).wait_recv()
            absorb(base + 1 - cc, i, False)
    hid[...] = (jax.nn.gelu(gacc[...], approximate=True) * uacc[...]).astype(BF16)

    for copy in w_copies[3]:
        copy.wait()
    precv_pairs = []
    for d in list(range(1, ny)) + [0]:
        yq = ahead(yy, d, ny)
        over = []
        for i, sp in enumerate(spans):
            core_s[d, :, sp] = mm(hid[...], down[yq * 2 + (1 - cc), :, sp], NN).astype(BF16)
            over.append(pltpu.make_async_remote_copy(
                src_ref=core_s.at[d, :, sp], dst_ref=core_r.at[d, :, sp],
                send_sem=c_ss.at[d, i], recv_sem=c_rs.at[d, i],
                device_id=(page, mate), device_id_type=MESH))
            over[i].start()
            sends.append(over[i])
        for i, sp in enumerate(spans):
            part = mm(hid[...], down[yq * 2 + cc, :, sp], NN)
            over[i].wait_recv()
            part = part + core_r[d, :, sp].astype(F32)
            if d:
                y_s[d - 1, :, sp] = part.astype(BF16)
                along = pltpu.make_async_remote_copy(
                    src_ref=y_s.at[d - 1, :, sp], dst_ref=y_r.at[d - 1, :, sp],
                    send_sem=y_ss.at[d - 1, i], recv_sem=y_rs.at[d - 1, i],
                    device_id=(page, yq * 2 + cc), device_id_type=MESH)
                along.start()
                sends.append(along)
                continue
            for e in range(1, ny):
                pltpu.make_async_remote_copy(
                    src_ref=y_s.at[e - 1, :, sp], dst_ref=y_r.at[e - 1, :, sp],
                    send_sem=y_ss.at[e - 1, i], recv_sem=y_rs.at[e - 1, i],
                    device_id=(page, mate), device_id_type=MESH).wait_recv()
                part = part + y_r[e - 1, :, sp].astype(F32)
            psend[:, :, sp] = part.reshape(n_page, BEAMS, sp.size).astype(BF16)
            precv[page, :, sp] = psend[page, :, sp]
            pair = page_copy(lambda p, sp=sp: psend.at[p, :, sp], lambda p, sp=sp: precv.at[p, :, sp],
                             p_ss.at[i], p_rs.at[i])
            pair[0]()
            precv_pairs.append(pair)
    for pair in precv_pairs:
        pair[1]()
    ff = jnp.sum(precv[...].astype(F32), axis=0)
    for g in range(n_feat):
        fsend[g] = ff[g * home:(g + 1) * home]
    frecv[feat] = fsend[feat]
    f_start, f_wait, f_done = feat_copy(
        lambda p: fsend.at[p], lambda p: frecv.at[p], lambda p: f_ss.at[p], lambda p: f_rs.at[p])
    f_start()
    f_wait()
    square = jnp.zeros((home, 1), F32)
    for c in range(n_feat):
        v = frecv[c]
        square += jnp.sum(v * v, axis=1, keepdims=True)
    scale = lax.rsqrt(square / depth + EPS)
    for c in range(n_feat):
        base = jnp.zeros((home, width), F32)
        r8 = res[c]
        for g in range(n_feat):
            base = jnp.where(feat == g, r8[g * home:(g + 1) * home], base)
        v = base + frecv[c] * scale * gain(2, c)
        out_ref[:, c * width:c * width + cut(c)] = v[:, 0:cut(c)].astype(BF16)

    q_done()
    st_done()
    n_done()
    lax.fori_loop(0, n_feat, lambda c, z: (pj(c)[2](), z)[1], 0)
    for i in range(parts):
        ag(i)[2]()
    for copy in sends:
        copy.wait_send()
    for pair in precv_pairs:
        pair[2]()
    f_done()


def per_device(
    n_page, n_feat,
    queries, fresh_keys, fresh_values, paged_keys, paged_values, block_tables, parents, prompt_lengths,
    stream, output_matrix, attention_gain, feedforward_gain, gate_matrix, linear_matrix, down_matrix, closing_gain,
):
    depth = stream.shape[1]
    home = stream.shape[0]
    tiles = -(-depth // 128)
    width = -(-tiles // n_feat) * 128
    padded = width * n_feat
    rows = n_page * queries.shape[0]
    slots, page_len, kvw = paged_keys.shape
    hw = queries.shape[1]
    units = gate_matrix.shape[0]
    ny = n_feat // 2
    sb = slots * BEAMS

    gains = jnp.concatenate([
        jnp.pad(g.astype(F32), (0, padded - depth)) if padded > depth else g.astype(F32)
        for g in (attention_gain, feedforward_gain, closing_gain)]).reshape(1, -1)

    parts = len(halves(width))
    dma = pltpu.SemaphoreType.DMA
    scratch = [
        pltpu.VMEM(paged_keys.shape, BF16), pltpu.VMEM(paged_values.shape, BF16),
        pltpu.VMEM((n_feat, width, hw), BF16),
        pltpu.VMEM((n_feat, units, width), BF16), pltpu.VMEM((n_feat, units, width), BF16),
        pltpu.VMEM((n_feat, units, width), BF16),
        pltpu.VMEM((n_page, BEAMS, hw), BF16),
        pltpu.VMEM((sb, hw), F32),
        pltpu.VMEM((sb, HEAD), F32),
        pltpu.VMEM((sb, hw), F32),
        pltpu.VMEM((sb, HEAD), F32),
        pltpu.VMEM((n_page, BEAMS, hw + HEAD), BF16),
        pltpu.VMEM((n_page, BEAMS, hw + HEAD), BF16),
        pltpu.VMEM((BEAMS, hw), BF16),
        pltpu.VMEM((n_feat, home, padded), F32),
        pltpu.VMEM((n_feat, n_feat, BEAMS, width), BF16),
        pltpu.VMEM((n_feat, BEAMS, width), F32),
        pltpu.VMEM((n_feat, n_page, BEAMS, width), BF16),
        pltpu.VMEM((rows, units), F32), pltpu.VMEM((rows, units), F32),
        pltpu.VMEM((rows, units), BF16),
        pltpu.VMEM((ny, rows, width), BF16), pltpu.VMEM((ny, rows, width), BF16),
        pltpu.VMEM((ny - 1, rows, width), BF16), pltpu.VMEM((ny - 1, rows, width), BF16),
        pltpu.VMEM((n_page, BEAMS, width), BF16), pltpu.VMEM((n_page, BEAMS, width), BF16),
        pltpu.VMEM((n_feat, home, width), F32), pltpu.VMEM((n_feat, home, width), F32),
        dma((2,)), dma((4, n_feat)),
        dma((n_page,)), dma((n_page,)),
        dma((n_page,)), dma((n_page,)),
        dma((n_feat,)), dma((n_feat,)),
        dma((n_feat, n_feat)), dma((n_feat, n_feat)),
        dma((parts, n_page)), dma((parts, n_page)),
        dma((ny, parts)), dma((ny, parts)), dma((n_feat, parts)),
        dma((ny, parts)), dma((ny, parts)), dma((ny - 1, parts)), dma((ny - 1, parts)),
        dma((parts, n_page)), dma((parts, n_page)),
        dma((n_feat,)), dma((n_feat,)),
    ]
    vmem = pl.BlockSpec(memory_space=pltpu.VMEM)
    hbm = pl.BlockSpec(memory_space=pl.ANY)
    return pl.pallas_call(
        functools.partial(layer_kernel, n_page, n_feat, width, depth),
        out_shape=jax.ShapeDtypeStruct((home, depth), BF16),
        in_specs=[vmem] * 8 + [hbm] * 6,
        out_specs=vmem,
        scratch_shapes=scratch,
        compiler_params=pltpu.CompilerParams(
            collective_id=0, has_side_effects=True, vmem_limit_bytes=60 * 2**20),
    )(queries, fresh_keys, fresh_values, block_tables.T, parents.reshape(1, -1),
      prompt_lengths.reshape(1, -1), stream, gains,
      paged_keys, paged_values, output_matrix, gate_matrix, linear_matrix, down_matrix)


def solution(mesh):
    both = P(("page", "feat"), None)
    placed = (
        P("page", "feat"), P("page", "feat"), P("page", "feat"),
        P("page", None, "feat"), P("page", None, "feat"),
        P(), P(), P(), both, P(None, "feat"), P(), P(), both, both, both, P(),
    )
    return jax.shard_map(
        functools.partial(per_device, mesh.shape["page"], mesh.shape["feat"]),
        mesh=mesh, in_specs=placed, out_specs=both, check_vma=False)
```

```python
import functools
import math

import jax
import jax.numpy as jnp
from jax import lax
from jax.experimental import pallas as pl
from jax.experimental.pallas import tpu as pltpu
from jax.sharding import PartitionSpec as P

HEAD = 128
QSCALAR = 144
SOFTCAP = 50
BEAMS = 8
EPS = 1e-06

F32 = jnp.float32
BF16 = jnp.bfloat16
MESH = pl.DeviceIdType.MESH
NT = (((1,), (1,)), ((), ()))
NN = (((1,), (0,)), ((), ()))
TN = (((0,), (0,)), ((), ()))


def capped_exp(raw):
    return jnp.exp(SOFTCAP * jnp.tanh(raw * (1.0 / (math.sqrt(QSCALAR) * SOFTCAP))))


def ahead(i, d, n):
    return jnp.where(i + d >= n, i + d - n, i + d)


def halves(width):
    first = width // 512 * 256
    return ((0, first), (first, width - first)) if first else ((0, width),)


def mm(a, b, dims):
    return lax.dot_general(a, b, dims, preferred_element_type=F32)


def layer_kernel(
    n_page, n_feat, width, depth,
    q_ref, fk_ref, fv_ref, tables_ref, parents_ref, lengths_ref, stream_ref, gains_ref,
    keys_hbm, values_hbm, wo_hbm, gate_hbm, lift_hbm, down_hbm,
    out_ref,
    kbuf, vbuf, wo, gate, lift, down,
    allq, qs, nvs, snum, stot, nsend, nrecv, att, strm, prj, res,
    xg, gacc, uacc, hid, core_s, core_r, y_s, y_r, psend, precv, fsend, frecv,
    kv_sem, w_sem,
    q_ss, q_rs, n_ss, n_rs, st_ss, st_rs, pj_ss, pj_rs, ag_ss, ag_rs,
    xy_ss, xc_ss, x_rs, c_ss, c_rs, y_ss, y_rs, p_ss, p_rs, f_ss, f_rs,
):
    page = lax.axis_index("page")
    feat = lax.axis_index("feat")
    ny = n_feat // 2
    yy, cc = feat // 2, feat % 2
    mate = yy * 2 + (1 - cc)
    slots, page_len, kvw = kbuf.shape
    kv_heads = kvw // HEAD
    heads = q_ref.shape[1] // HEAD
    groups = heads // kv_heads
    rows = n_page * BEAMS
    home = stream_ref.shape[0]
    hw = heads * HEAD

    spans = [pl.ds(first, size) for first, size in halves(width)]
    parts = len(spans)

    def gain(i, c):
        first = (i * n_feat + c) * width
        return gains_ref[:, first:first + width]

    def cut(c):
        return min(width, depth - c * width)

    local = [
        pltpu.make_async_copy(keys_hbm, kbuf, kv_sem.at[0]),
        pltpu.make_async_copy(values_hbm, vbuf, kv_sem.at[1]),
    ]
    w_copies = [[], [], [], []]
    for c in range(n_feat):
        part = pl.ds(c * width, cut(c))
        have = pl.ds(0, cut(c))
        w_copies[0].append(pltpu.make_async_copy(wo_hbm.at[part, :], wo.at[c, have, :], w_sem.at[0, c]))
        w_copies[1].append(pltpu.make_async_copy(gate_hbm.at[:, part], gate.at[c, :, have], w_sem.at[1, c]))
        w_copies[2].append(pltpu.make_async_copy(lift_hbm.at[:, part], lift.at[c, :, have], w_sem.at[2, c]))
        w_copies[3].append(pltpu.make_async_copy(down_hbm.at[:, part], down.at[c, :, have], w_sem.at[3, c]))
        if cut(c) < width:
            rest = width - cut(c)
            wo[c, cut(c):, :] = jnp.zeros((rest, wo.shape[2]), BF16)
            gate[c, :, cut(c):] = jnp.zeros((gate.shape[1], rest), BF16)
            lift[c, :, cut(c):] = jnp.zeros((gate.shape[1], rest), BF16)
            down[c, :, cut(c):] = jnp.zeros((gate.shape[1], rest), BF16)
    for copy in local:
        copy.start()

    barrier = pltpu.get_barrier_semaphore()

    def greet_page(d, _):
        pl.semaphore_signal(barrier, inc=1, device_id=(ahead(page, d, n_page), feat), device_id_type=MESH)
        return 0

    def greet_feat(d, _):
        pl.semaphore_signal(barrier, inc=1, device_id=(page, ahead(feat, d, n_feat)), device_id_type=MESH)
        return 0

    lax.fori_loop(1, n_page, greet_page, 0)
    lax.fori_loop(1, n_feat, greet_feat, 0)

    allq[page] = q_ref[...]
    sf = stream_ref[...].astype(F32)
    if strm.shape[2] > depth:
        sf = jnp.concatenate([sf, jnp.zeros((home, strm.shape[2] - depth), F32)], axis=1)
    strm[feat] = sf
    pl.semaphore_wait(barrier, n_page + n_feat - 2)

    def page_copy(src, dst, ss, rs):
        def send(d):
            peer = ahead(page, d, n_page)
            return pltpu.make_async_remote_copy(
                src_ref=src(peer), dst_ref=dst(page), send_sem=ss.at[peer], recv_sem=rs.at[page],
                device_id=(peer, feat), device_id_type=MESH)

        def arrival(d):
            peer = ahead(page, d, n_page)
            return pltpu.make_async_remote_copy(
                src_ref=src(peer), dst_ref=dst(peer), send_sem=ss.at[peer], recv_sem=rs.at[peer],
                device_id=(peer, feat), device_id_type=MESH)

        def start():
            lax.fori_loop(1, n_page, lambda d, z: (send(d).start(), z)[1], 0, unroll=n_page <= 8)

        def wait_recv():
            lax.fori_loop(1, n_page, lambda d, z: (arrival(d).wait_recv(), z)[1], 0, unroll=n_page <= 8)

        def wait_send():
            lax.fori_loop(1, n_page, lambda d, z: (send(d).wait_send(), z)[1], 0, unroll=n_page <= 8)

        return start, wait_recv, wait_send

    def feat_copy(src, dst, ss, rs):
        def send(d):
            peer = ahead(feat, d, n_feat)
            return pltpu.make_async_remote_copy(
                src_ref=src(peer), dst_ref=dst(feat), send_sem=ss(peer), recv_sem=rs(feat),
                device_id=(page, peer), device_id_type=MESH)

        def arrival(d):
            peer = ahead(feat, d, n_feat)
            return pltpu.make_async_remote_copy(
                src_ref=src(peer), dst_ref=dst(peer), send_sem=ss(peer), recv_sem=rs(peer),
                device_id=(page, peer), device_id_type=MESH)

        def start():
            lax.fori_loop(1, n_feat, lambda d, z: (send(d).start(), z)[1], 0, unroll=n_feat <= 8)

        def wait_recv():
            lax.fori_loop(1, n_feat, lambda d, z: (arrival(d).wait_recv(), z)[1], 0, unroll=n_feat <= 8)

        def wait_send():
            lax.fori_loop(1, n_feat, lambda d, z: (send(d).wait_send(), z)[1], 0, unroll=n_feat <= 8)

        return start, wait_recv, wait_send

    q_start, q_wait, q_done = page_copy(lambda p: allq.at[page], lambda p: allq.at[p], q_ss, q_rs)
    q_start()
    st_start, st_wait, st_done = feat_copy(
        lambda p: strm.at[feat], lambda p: strm.at[p], lambda p: st_ss.at[p], lambda p: st_rs.at[p])
    st_start()

    blocks = tables_ref.shape[0]
    prompts = lengths_ref.shape[1]
    sb = slots * BEAMS
    chosen = lax.broadcasted_iota(jnp.int32, (rows, rows), 0) == parents_ref[...]
    by_col = lax.dot_general(tables_ref[...].astype(F32), jnp.where(chosen, 1.0, 0.0), NN,
                             precision=lax.Precision.HIGHEST, preferred_element_type=F32)
    of_prompt = (lax.broadcasted_iota(jnp.int32, (prompts, rows), 0)
                 == lax.broadcasted_iota(jnp.int32, (prompts, rows), 1) // BEAMS)
    lens = lax.dot_general(lengths_ref[...].astype(F32), jnp.where(of_prompt, 1.0, 0.0), NN,
                           precision=lax.Precision.HIGHEST, preferred_element_type=F32)
    spot_i = lax.broadcasted_iota(jnp.int32, (sb, rows), 0)
    row_i = lax.broadcasted_iota(jnp.int32, (sb, rows), 1)
    slot_id = (page * slots + spot_i // BEAMS).astype(F32)
    seen = jnp.zeros((sb, rows), F32)
    for b in range(blocks):
        seen += jnp.where(jnp.abs(by_col[b:b + 1, :] - slot_id) < 0.5,
                          jnp.clip(lens - b * page_len, 0.0, float(page_len)), 0.0)
    seen = jnp.where(spot_i % BEAMS == row_i % BEAMS, seen, 0.0)
    pick = jnp.where(seen > 0, 1.0, 0.0).astype(BF16)
    nvs[...] = jnp.broadcast_to(jnp.sum(seen, axis=1, keepdims=True), nvs.shape)

    q_wait()
    q_all = allq[...].astype(F32).reshape(rows, hw).astype(BF16)
    qs[...] = mm(pick, q_all, NN)
    for copy in local:
        copy.wait()
    for kind in w_copies:
        for copy in kind:
            copy.start()

    half_lanes = HEAD // 2
    pair = 2 if kv_heads % 2 == 0 else 1
    sets = kv_heads // pair
    ph = pair * groups
    pw = ph * HEAD
    lane = lax.broadcasted_iota(jnp.int32, (BEAMS, HEAD), 1)
    position = lax.broadcasted_iota(jnp.int32, (ph * BEAMS, page_len), 1).astype(F32)
    nothing = jnp.zeros((BEAMS, HEAD), F32)

    def one_slot(s, t):
        at = pl.ds(pl.multiple_of(s * BEAMS, BEAMS), BEAMS)
        visible = position < jnp.concatenate([nvs[at, :]] * ph, axis=0)[:, 0:1]
        qk = []
        for i in range(ph):
            h = t * ph + i
            piece = qs[at, h * HEAD:(h + 1) * HEAD]
            qk.append(jnp.concatenate([piece if j == i // groups else nothing for j in range(pair)], axis=1))
        kv = slice(t * pair * HEAD, (t + 1) * pair * HEAD)
        raw = mm(jnp.concatenate(qk, axis=0).astype(BF16), kbuf[s, :, kv], NT)
        w = jnp.where(visible, capped_exp(raw), 0.0)
        tot = jnp.sum(w, axis=1, keepdims=True)
        num = mm(w.astype(BF16), vbuf[s, :, kv], NN)
        sums = nothing
        for i in range(ph):
            h, k = t * ph + i, i // groups
            own = slice(i * BEAMS, (i + 1) * BEAMS)
            snum[at, h * HEAD:(h + 1) * HEAD] = num[own, k * HEAD:(k + 1) * HEAD]
            sums = jnp.where(lane % half_lanes == i, tot[own], sums)
        stot[t, at, :] = sums

    per = 8 if slots % 8 == 0 else 1

    def to_rows(v):
        hi = v.astype(BF16)
        lo = (v - hi.astype(F32)).astype(BF16)
        return mm(pick, hi, TN) + mm(pick, lo, TN)

    def n_copy(t):
        return page_copy(lambda p: nsend.at[t, p], lambda p: nrecv.at[t, p], n_ss.at[t], n_rs.at[t])

    for t in range(sets):
        def some_slots(i, z, t=t):
            for u in range(per):
                one_slot(i * per + u, t)
            return z

        lax.fori_loop(0, slots // per, some_slots, 0)
        tot_rows = to_rows(stot[t])
        tot_hi = tot_rows.astype(BF16).astype(F32)
        first = lax.broadcasted_iota(jnp.int32, tot_rows.shape, 1) < half_lanes
        tot_both = jnp.where(first, tot_hi, tot_rows - tot_hi)
        nsend[t, :, :, 0:pw] = to_rows(snum[:, t * pw:(t + 1) * pw]).reshape(n_page, BEAMS, pw).astype(BF16)
        nsend[t, :, :, pw:pw + HEAD] = tot_both.reshape(n_page, BEAMS, HEAD).astype(BF16)
        nrecv[t, page] = nsend[t, page]
        n_copy(t)[0]()

    own_w = []
    for h in range(heads):
        k = h // groups
        qk = q_ref[:, h * HEAD:(h + 1) * HEAD].astype(F32) * fk_ref[:, k * HEAD:(k + 1) * HEAD].astype(F32)
        own_w.append(capped_exp(jnp.sum(qk, axis=1, keepdims=True)))
    for copy in w_copies[0]:
        copy.wait()

    def pj(c):
        return feat_copy(lambda p: prj.at[feat, c], lambda p: prj.at[p, c],
                         lambda p: pj_ss.at[p, c], lambda p: pj_rs.at[p, c])

    for t in range(sets):
        n_copy(t)[1]()
        totals = jnp.sum(nrecv[t, :, :, pw:pw + HEAD].astype(F32), axis=0)
        for i in range(ph):
            h = t * ph + i
            k = h // groups
            num = jnp.sum(nrecv[t, :, :, i * HEAD:(i + 1) * HEAD].astype(F32), axis=0)
            num += own_w[h].astype(BF16).astype(F32) * fv_ref[:, k * HEAD:(k + 1) * HEAD].astype(F32)
            total = totals[:, i:i + 1] + totals[:, half_lanes + i:half_lanes + i + 1] + own_w[h]
            att[:, h * HEAD:(h + 1) * HEAD] = (num / total).astype(BF16)

        def project(c, z, t=t):
            v = mm(att[:, t * pw:(t + 1) * pw], wo[c, :, t * pw:(t + 1) * pw], NT)
            if t:
                v += res[c]
            if t < sets - 1:
                res[c] = v
            else:
                prj[feat, c] = v.astype(BF16)
                pj(c)[0]()
            return z

        lax.fori_loop(0, n_feat, project, 0)
    st_wait()
    lax.fori_loop(0, n_feat, lambda c, z: (pj(c)[1](), z)[1], 0)

    square = jnp.zeros((BEAMS, 1), F32)
    for c in range(n_feat):
        v = jnp.sum(prj[:, c].astype(F32), axis=0)
        res[c] = v
        square += jnp.sum(v * v, axis=1, keepdims=True)
    scale = lax.rsqrt(square / depth + EPS)
    square = jnp.zeros((BEAMS, 1), F32)
    for c in range(n_feat):
        cols = slice(c * width, (c + 1) * width)
        base = jnp.concatenate([strm[g, :, cols] for g in range(n_feat)], axis=0)
        v = base + res[c] * scale * gain(0, c)
        res[c] = v
        square += jnp.sum(v * v, axis=1, keepdims=True)
    scale = lax.rsqrt(square / depth + EPS)
    own_gain = gain(1, 0)
    for c in range(1, n_feat):
        own_gain = jnp.where(feat == c, gain(1, c), own_gain)
    xg[feat, page] = (res[feat] * scale * own_gain).astype(BF16)

    def ag(i):
        return page_copy(lambda p: xg.at[feat, page, :, spans[i]], lambda p: xg.at[feat, p, :, spans[i]],
                         ag_ss.at[i], ag_rs.at[i])

    for i in range(parts):
        ag(i)[0]()
    for kind in w_copies[1:3]:
        for copy in kind:
            copy.wait()

    def chunk_copy(q, i, peer, ss):
        return pltpu.make_async_remote_copy(
            src_ref=xg.at[q, :, :, spans[i]], dst_ref=xg.at[q, :, :, spans[i]], send_sem=ss, recv_sem=x_rs.at[q, i],
            device_id=(page, peer), device_id_type=MESH)

    sends = []

    def absorb(q, i, fresh):
        sp = spans[i]
        x = xg[q, :, :, sp].astype(F32).reshape(rows, sp.size).astype(BF16)
        if fresh:
            gacc[...] = mm(x, gate[q, :, sp], NT)
            uacc[...] = mm(x, lift[q, :, sp], NT)
        else:
            gacc[...] += mm(x, gate[q, :, sp], NT)
            uacc[...] += mm(x, lift[q, :, sp], NT)

    for i in range(parts):
        ag(i)[1]()
        for d in range(1, ny):
            sends.append(chunk_copy(feat, i, ahead(yy, d, ny) * 2 + cc, xy_ss.at[d, i]))
            sends[-1].start()
        sends.append(chunk_copy(feat, i, mate, xc_ss.at[0, i]))
        sends[-1].start()
        absorb(feat, i, i == 0)
    for i in range(parts):
        chunk_copy(mate, i, mate, xc_ss.at[0, i]).wait_recv()
        absorb(mate, i, False)
    for d in range(1, ny):
        base = ahead(yy, ny - d, ny) * 2
        for i in range(parts):
            chunk_copy(base + cc, i, mate, xc_ss.at[d, i]).wait_recv()
            sends.append(chunk_copy(base + cc, i, mate, xc_ss.at[d, i]))
            sends[-1].start()
            absorb(base + cc, i, False)
        for i in range(parts):
            chunk_copy(base + 1 - cc, i, mate, xc_ss.at[d, i]).wait_recv()
            absorb(base + 1 - cc, i, False)
    hid[...] = (jax.nn.gelu(gacc[...], approximate=True) * uacc[...]).astype(BF16)

    for copy in w_copies[3]:
        copy.wait()
    precv_pairs = []
    for d in list(range(1, ny)) + [0]:
        yq = ahead(yy, d, ny)
        over = []
        for i, sp in enumerate(spans):
            core_s[d, :, sp] = mm(hid[...], down[yq * 2 + (1 - cc), :, sp], NN).astype(BF16)
            over.append(pltpu.make_async_remote_copy(
                src_ref=core_s.at[d, :, sp], dst_ref=core_r.at[d, :, sp],
                send_sem=c_ss.at[d, i], recv_sem=c_rs.at[d, i],
                device_id=(page, mate), device_id_type=MESH))
            over[i].start()
            sends.append(over[i])
        for i, sp in enumerate(spans):
            part = mm(hid[...], down[yq * 2 + cc, :, sp], NN)
            over[i].wait_recv()
            part = part + core_r[d, :, sp].astype(F32)
            if d:
                y_s[d - 1, :, sp] = part.astype(BF16)
                along = pltpu.make_async_remote_copy(
                    src_ref=y_s.at[d - 1, :, sp], dst_ref=y_r.at[d - 1, :, sp],
                    send_sem=y_ss.at[d - 1, i], recv_sem=y_rs.at[d - 1, i],
                    device_id=(page, yq * 2 + cc), device_id_type=MESH)
                along.start()
                sends.append(along)
                continue
            for e in range(1, ny):
                pltpu.make_async_remote_copy(
                    src_ref=y_s.at[e - 1, :, sp], dst_ref=y_r.at[e - 1, :, sp],
                    send_sem=y_ss.at[e - 1, i], recv_sem=y_rs.at[e - 1, i],
                    device_id=(page, mate), device_id_type=MESH).wait_recv()
                part = part + y_r[e - 1, :, sp].astype(F32)
            psend[:, :, sp] = part.reshape(n_page, BEAMS, sp.size).astype(BF16)
            precv[page, :, sp] = psend[page, :, sp]
            pair = page_copy(lambda p, sp=sp: psend.at[p, :, sp], lambda p, sp=sp: precv.at[p, :, sp],
                             p_ss.at[i], p_rs.at[i])
            pair[0]()
            precv_pairs.append(pair)
    for pair in precv_pairs:
        pair[1]()
    ff = jnp.sum(precv[...].astype(F32), axis=0)
    for g in range(n_feat):
        fsend[g] = ff[g * home:(g + 1) * home]
    frecv[feat] = fsend[feat]
    f_start, f_wait, f_done = feat_copy(
        lambda p: fsend.at[p], lambda p: frecv.at[p], lambda p: f_ss.at[p], lambda p: f_rs.at[p])
    f_start()
    f_wait()
    square = jnp.zeros((home, 1), F32)
    for c in range(n_feat):
        v = frecv[c]
        square += jnp.sum(v * v, axis=1, keepdims=True)
    scale = lax.rsqrt(square / depth + EPS)
    for c in range(n_feat):
        base = jnp.zeros((home, width), F32)
        r8 = res[c]
        for g in range(n_feat):
            base = jnp.where(feat == g, r8[g * home:(g + 1) * home], base)
        v = base + frecv[c] * scale * gain(2, c)
        out_ref[:, c * width:c * width + cut(c)] = v[:, 0:cut(c)].astype(BF16)

    q_done()
    st_done()
    for t in range(sets):
        n_copy(t)[2]()
    lax.fori_loop(0, n_feat, lambda c, z: (pj(c)[2](), z)[1], 0)
    for i in range(parts):
        ag(i)[2]()
    for copy in sends:
        copy.wait_send()
    for pair in precv_pairs:
        pair[2]()
    f_done()


def per_device(
    n_page, n_feat,
    queries, fresh_keys, fresh_values, paged_keys, paged_values, block_tables, parents, prompt_lengths,
    stream, output_matrix, attention_gain, feedforward_gain, gate_matrix, linear_matrix, down_matrix, closing_gain,
):
    depth = stream.shape[1]
    home = stream.shape[0]
    tiles = -(-depth // 128)
    width = -(-tiles // n_feat) * 128
    padded = width * n_feat
    rows = n_page * queries.shape[0]
    slots, page_len, kvw = paged_keys.shape
    hw = queries.shape[1]
    units = gate_matrix.shape[0]
    ny = n_feat // 2
    sb = slots * BEAMS

    gains = jnp.concatenate([
        jnp.pad(g.astype(F32), (0, padded - depth)) if padded > depth else g.astype(F32)
        for g in (attention_gain, feedforward_gain, closing_gain)]).reshape(1, -1)

    kv_heads = kvw // HEAD
    sets = kv_heads // 2 if kv_heads % 2 == 0 else kv_heads
    parts = len(halves(width))
    dma = pltpu.SemaphoreType.DMA
    scratch = [
        pltpu.VMEM(paged_keys.shape, BF16), pltpu.VMEM(paged_values.shape, BF16),
        pltpu.VMEM((n_feat, width, hw), BF16),
        pltpu.VMEM((n_feat, units, width), BF16), pltpu.VMEM((n_feat, units, width), BF16),
        pltpu.VMEM((n_feat, units, width), BF16),
        pltpu.VMEM((n_page, BEAMS, hw), BF16),
        pltpu.VMEM((sb, hw), F32),
        pltpu.VMEM((sb, HEAD), F32),
        pltpu.VMEM((sb, hw), F32),
        pltpu.VMEM((sets, sb, HEAD), F32),
        pltpu.VMEM((sets, n_page, BEAMS, hw // sets + HEAD), BF16),
        pltpu.VMEM((sets, n_page, BEAMS, hw // sets + HEAD), BF16),
        pltpu.VMEM((BEAMS, hw), BF16),
        pltpu.VMEM((n_feat, home, padded), F32),
        pltpu.VMEM((n_feat, n_feat, BEAMS, width), BF16),
        pltpu.VMEM((n_feat, BEAMS, width), F32),
        pltpu.VMEM((n_feat, n_page, BEAMS, width), BF16),
        pltpu.VMEM((rows, units), F32), pltpu.VMEM((rows, units), F32),
        pltpu.VMEM((rows, units), BF16),
        pltpu.VMEM((ny, rows, width), BF16), pltpu.VMEM((ny, rows, width), BF16),
        pltpu.VMEM((ny - 1, rows, width), BF16), pltpu.VMEM((ny - 1, rows, width), BF16),
        pltpu.VMEM((n_page, BEAMS, width), BF16), pltpu.VMEM((n_page, BEAMS, width), BF16),
        pltpu.VMEM((n_feat, home, width), F32), pltpu.VMEM((n_feat, home, width), F32),
        dma((2,)), dma((4, n_feat)),
        dma((n_page,)), dma((n_page,)),
        dma((sets, n_page)), dma((sets, n_page)),
        dma((n_feat,)), dma((n_feat,)),
        dma((n_feat, n_feat)), dma((n_feat, n_feat)),
        dma((parts, n_page)), dma((parts, n_page)),
        dma((ny, parts)), dma((ny, parts)), dma((n_feat, parts)),
        dma((ny, parts)), dma((ny, parts)), dma((ny - 1, parts)), dma((ny - 1, parts)),
        dma((parts, n_page)), dma((parts, n_page)),
        dma((n_feat,)), dma((n_feat,)),
    ]
    vmem = pl.BlockSpec(memory_space=pltpu.VMEM)
    hbm = pl.BlockSpec(memory_space=pl.ANY)
    return pl.pallas_call(
        functools.partial(layer_kernel, n_page, n_feat, width, depth),
        out_shape=jax.ShapeDtypeStruct((home, depth), BF16),
        in_specs=[vmem] * 8 + [hbm] * 6,
        out_specs=vmem,
        scratch_shapes=scratch,
        compiler_params=pltpu.CompilerParams(
            collective_id=0, has_side_effects=True, vmem_limit_bytes=60 * 2**20),
    )(queries, fresh_keys, fresh_values, block_tables.T, parents.reshape(1, -1),
      prompt_lengths.reshape(1, -1), stream, gains,
      paged_keys, paged_values, output_matrix, gate_matrix, linear_matrix, down_matrix)


def solution(mesh):
    both = P(("page", "feat"), None)
    placed = (
        P("page", "feat"), P("page", "feat"), P("page", "feat"),
        P("page", None, "feat"), P("page", None, "feat"),
        P(), P(), P(), both, P(None, "feat"), P(), P(), both, both, both, P(),
    )
    return jax.shard_map(
        functools.partial(per_device, mesh.shape["page"], mesh.shape["feat"]),
        mesh=mesh, in_specs=placed, out_specs=both, check_vma=False)
```
